1024 devices in a mesh: dp: 64 (over y, x, core), fsdp: 16 (over z).
Axes of the slice: x: 4, y: 8, z: 16, core: 2. Of those that a mesh axis runs over, the one named last changes fastest.
Arguments:
- grad_partial: bfloat16 [64, 16, 64, 2048], P('dp', None, None, 'fsdp'), may hold values from -16 to 16
- weights: bfloat16 [16, 64, 2048], P(None, None, 'fsdp'), may hold values from -0.59765625 to 0.59765625
- momentum: float32 [16, 4, 64, 2048], P('fsdp'), may hold values from -6 to 6
- owners: int32 [16], replicated, may hold values from 0 to 15, as said below
Outputs:
- weights_out: bfloat16 [16, 64, 2048], replicated
- momentum_out: float32 [16, 4, 64, 2048], P('fsdp')
The draws below stay inside these ranges and needn't reach their ends.
Inputs may be any that keep to these rules, and one draw needn't show every extreme that they name: `owners`: no owner holds more than 4 matrices, and one owner holds exactly 4.
All inputs are finite; a program needn't handle non-finite values.
Results may differ from the reference program's by a relative error of at most 0.013.
Values may be sent and summed in bfloat16 or wider, within the bound.
No kernel may reach another device: no remote copies, remote signals or barrier semaphores. Data moves between devices by JAX's collectives and lax.ppermute only.
A program may use at most 32 MiB of HBM per device.

```python
import jax
import jax.numpy as jnp
from jax import lax

E = 64
D = 2048
L = 16
MAXOWN = 4
ITERS = 5
N_DP = 64
N_FSDP = 16


def draw_grad_partial(key, part):
    key = jax.random.fold_in(key, 11)
    row_key, col_key, noise_key = jax.random.split(key, 3)
    row_scale = jnp.exp(jax.random.uniform(row_key, (1, L, E, 1), jnp.float32, 0.0, jnp.log(10.0)))
    col_scale = jnp.exp(jax.random.uniform(col_key, (1, L, 1, D), jnp.float32, 0.0, jnp.log(10.0)))
    term = jnp.clip(jax.random.normal(noise_key, (N_DP, L, E, D), jnp.float32), -4.0, 4.0)
    values = term * row_scale * col_scale / (10.0 * N_DP ** 0.5)
    return values.astype(jnp.bfloat16)


def draw_owners(key, part):
    key = jax.random.fold_in(key, 5)
    full_key, other_key, order_key = jax.random.split(key, 3)
    fullest = jax.random.randint(full_key, (), 0, N_FSDP)
    others = jax.random.permutation(other_key, (N_FSDP - 1) * MAXOWN)[:L - MAXOWN] // MAXOWN
    others = others + (others >= fullest).astype(others.dtype)
    listed = jnp.concatenate([jnp.full((MAXOWN,), fullest, dtype=others.dtype), others])
    shuffle = jax.random.permutation(order_key, L)
    return listed[shuffle].astype(jnp.int32)


def levels(key, extent, pieces, least, top_value):
    def one(dim, shards_of):
        heights = jax.random.uniform(jax.random.fold_in(jax.random.fold_in(key, 6), dim), (shards_of,), jnp.float32, least / len(pieces), top_value / len(pieces))
        return jnp.repeat(jnp.exp(heights), extent[dim] // shards_of).reshape((-1,) + (1,) * (len(extent) - dim - 1))

    gain = one(*pieces[0])
    for cut in pieces[1:]:
        gain = gain * one(*cut)
    return gain


def gaussian(key, dims, scale, most, cuts=(), held_as=jnp.bfloat16):
    level = levels(key, dims, cuts, -0.22, 0.18) if cuts else 1.0
    entries = jax.random.normal(key, dims, jnp.float32) * scale * level
    return jnp.minimum(jnp.maximum(entries, -most), most).astype(held_as)


def setup_inputs(seed: int = 0) -> dict:
    arg_keys = jax.random.split(jax.random.key(seed), 5)
    grad_partial = draw_grad_partial(jax.random.fold_in(arg_keys[4], 71), 0)
    weights = gaussian(arg_keys[1], (L, E, D), 0.1, 0.59765625, ((2, 16),))
    momentum = gaussian(arg_keys[2], (N_FSDP, MAXOWN, E, D), 1.0, 6.0, ((0, 16),), jnp.float32)
    owners = draw_owners(jax.random.fold_in(arg_keys[4], 71), 0)
    return dict(grad_partial=grad_partial, weights=weights, momentum=momentum, owners=owners)


coef_a = 3.4445
coef_b = -4.775
coef_c = 2.0315
moment_rate = 0.95
learn_rate = 0.1
decay_rate = 0.1

def slot_numbers(owners):
    table = (owners[:, None] == jnp.arange(N_FSDP, dtype=jnp.int32)[None, :]).astype(jnp.int32)
    before = jnp.cumsum(table, axis=0) - table
    return lax.optimization_barrier(jnp.sum(before * table, axis=1)).astype(jnp.int32)

def orthogonalize(initial):
    frobenius = jnp.sqrt(jnp.sum(initial * initial))
    current = (initial / (frobenius + 1e-07)).astype(jnp.bfloat16)
    for repeat in range(ITERS):
        gram_matrix = jnp.dot(current, current.T, preferred_element_type=jnp.float32).astype(jnp.bfloat16)
        square = jnp.dot(gram_matrix, gram_matrix, preferred_element_type=jnp.float32)
        polynomial = (coef_b * gram_matrix.astype(jnp.float32) + coef_c * square).astype(jnp.bfloat16)
        current = (coef_a * current.astype(jnp.float32) + jnp.dot(polynomial, current, preferred_element_type=jnp.float32)).astype(jnp.bfloat16)
    return current

def reference(grad_partial, weights, momentum, owners):
    summed = lax.optimization_barrier(jnp.sum(grad_partial, axis=0, dtype=jnp.float32)).astype(jnp.bfloat16)
    slot = slot_numbers(owners)
    previous = momentum[owners, slot]
    moment = moment_rate * previous + summed.astype(jnp.float32)
    initial = summed.astype(jnp.float32) + moment_rate * moment
    ortho = lax.map(orthogonalize, initial)
    scale = 0.2 * D ** 0.5
    wide = weights.astype(jnp.float32)
    weights_out = (wide - learn_rate * (scale * ortho.astype(jnp.float32) + decay_rate * wide)).astype(jnp.bfloat16)
    momentum_out = jnp.zeros((N_FSDP, MAXOWN, E, D), jnp.float32).at[owners, slot].set(moment)
    return (weights_out, momentum_out)
```

```python
import jax
import jax.numpy as jnp
from jax import lax
from jax.experimental import pallas as pl
from jax.experimental.pallas import tpu as pltpu
from jax.sharding import Mesh, PartitionSpec as P

E = 64
D = 2048
L = 16
DEPTH = 4
ITERS = 5
NY, NX, NC, NZ = 8, 4, 2, 16
HALF = L // NC
RG = 4
ROWS = E // RG
COLS = D // NZ
GROUP = 4 * E
DP = ("y", "x", "core")
Z = "fsdp"

coef_a = 3.4445
coef_b = -4.775
coef_c = 2.0315
moment_rate = 0.95
learn_rate = 0.1
decay_rate = 0.1
scale = 0.2 * D**0.5
INIT_S = 1.0 + moment_rate
INIT_M = moment_rate * moment_rate
BACK_I = 1.0 / INIT_S
BACK_M = moment_rate - INIT_M / INIT_S


def ortho_kernel(x_ref, w_ref, o_ref, xs):
    for l in range(HALF):
        for z in range(NZ):
            xs[l * E : (l + 1) * E, z * COLS : (z + 1) * COLS] = x_ref[l, :, z].reshape(E, COLS)
    row = lax.broadcasted_iota(jnp.int32, (GROUP, GROUP), 0)
    col = lax.broadcasted_iota(jnp.int32, (GROUP, GROUP), 1)
    same = (row >> 6) == (col >> 6)
    diagonal = row == col
    eye_a = jnp.where(diagonal, coef_a, 0.0)

    def mm(a, b):
        return jnp.dot(a, b, precision=lax.Precision.HIGHEST, preferred_element_type=jnp.float32)

    groups = range(HALF * E // GROUP)
    grams, scales = [], []
    for g in groups:
        x = xs[g * GROUP : (g + 1) * GROUP, :]
        gram = lax.dot_general(
            x, x, (((1,), (1,)), ((), ())), preferred_element_type=jnp.float32
        )
        trace = jnp.where(diagonal, gram, 0.0)
        by_row = jnp.sum(trace, axis=1, keepdims=True)
        by_col = jnp.sum(trace, axis=0, keepdims=True)
        total_row = jnp.sum(jnp.where(same, by_col, 0.0), axis=1, keepdims=True)
        total_col = jnp.sum(jnp.where(same, by_row, 0.0), axis=0, keepdims=True)
        inv_row = 1.0 / (jnp.sqrt(total_row) + 1e-07)
        inv_col = 1.0 / (jnp.sqrt(total_col) + 1e-07)
        grams.append(jnp.where(same, gram * inv_row * inv_col, 0.0))
        scales.append(inv_col)
    polys = [None for _ in groups]
    for repeat in range(ITERS):
        squares = [mm(gram, gram) for gram in grams]
        steps = [eye_a + coef_b * gram + coef_c * sq for gram, sq in zip(grams, squares)]
        polys = [
            step if poly is None else mm(step, poly) for step, poly in zip(steps, polys)
        ]
        if repeat < ITERS - 1:
            halfway = [mm(step, gram) for step, gram in zip(steps, grams)]
            grams = [mm(half, step) for half, step in zip(halfway, steps)]
    for g in groups:
        poly = polys[g] * scales[g]
        high = poly.astype(jnp.bfloat16)
        low = (poly - high.astype(jnp.float32)).astype(jnp.bfloat16)
        for z in range(NZ // 2):
            x = xs[g * GROUP : (g + 1) * GROUP, 2 * z * COLS : 2 * (z + 1) * COLS]
            ortho = jnp.dot(high, x, preferred_element_type=jnp.float32) + jnp.dot(
                low, x, preferred_element_type=jnp.float32
            )
            for part in range(2):
                k = 2 * z + part
                wide = w_ref[k, 4 * g : 4 * (g + 1)].reshape(GROUP, COLS).astype(jnp.float32)
                mine = ortho[:, part * COLS : (part + 1) * COLS]
                new = wide - learn_rate * (scale * mine + decay_rate * wide)
                new = new.astype(jnp.bfloat16).reshape(4, E, COLS)
                for copy in range(NC):
                    o_ref[copy, 4 * g : 4 * (g + 1), :, k * COLS : (k + 1) * COLS] = new


def update_weights(x, weights):
    return pl.pallas_call(
        ortho_kernel,
        out_shape=jax.ShapeDtypeStruct((NC, HALF, E, D), jnp.bfloat16),
        in_specs=[pl.BlockSpec(memory_space=pltpu.VMEM)] * 2,
        out_specs=pl.BlockSpec(memory_space=pltpu.VMEM),
        scratch_shapes=[pltpu.VMEM((HALF * E, D), jnp.bfloat16)],
        compiler_params=pltpu.CompilerParams(vmem_limit_bytes=40 * 2**20),
        cost_estimate=pl.CostEstimate(
            flops=2 * 10**10, bytes_accessed=8 * 2**20, transcendentals=0
        ),
        name="update_weights",
    )(x, weights)


def moment_kernel(present_ref, near_ref, far_ref, m_ref, o_ref):
    here = present_ref[pl.program_id(0)] > 0
    for z in range(NZ):
        columns = pl.ds(z * COLS, COLS)
        initial = near_ref[0, :, z].astype(jnp.float32) + far_ref[0, :, z].astype(jnp.float32)
        moment = BACK_I * initial.reshape(E, COLS) + BACK_M * m_ref[0, :, columns]
        o_ref[0, :, columns] = jnp.where(here, moment, 0.0)


def update_momentum(present, near, far, momentum):
    picked = pl.BlockSpec((1, RG, NZ, ROWS, COLS), lambda s, p: (s, 0, 0, 0, 0))
    whole = pl.BlockSpec((1, E, D), lambda s, p: (s, 0, 0))
    return pl.pallas_call(
        moment_kernel,
        out_shape=jax.ShapeDtypeStruct((DEPTH, E, D), jnp.float32),
        grid_spec=pltpu.PrefetchScalarGridSpec(
            num_scalar_prefetch=1,
            grid=(DEPTH,),
            in_specs=[picked, picked, whole],
            out_specs=whole,
        ),
        name="update_momentum",
    )(present, near, far, momentum)


def spread(x, axis, count):
    return lax.all_to_all(jnp.broadcast_to(x[None], (count,) + x.shape), axis, 0, 0, tiled=True)


def local(grad_partial, weights, momentum, owners):
    y, x, core = lax.axis_index("y"), lax.axis_index("x"), lax.axis_index("core")
    own_index = lax.axis_index(Z)
    layers = jnp.arange(L, dtype=jnp.int32)
    first = HALF * core
    slots = jnp.sum(
        ((owners[None, :] == owners[:, None]) & (layers[None, :] < layers[:, None])).astype(
            jnp.int32
        ),
        axis=1,
    )

    kept = lax.dynamic_slice_in_dim(weights, first, HALF, 0)
    weights_half = lax.all_gather(kept, Z)

    my_layer = first + 2 * x + y // RG
    my_rows = (y % RG) * ROWS
    my_owner = lax.dynamic_index_in_dim(owners, my_layer, 0, keepdims=False)
    my_slot = lax.dynamic_index_in_dim(slots, my_layer, 0, keepdims=False)

    held = lax.dynamic_slice(momentum[0], (my_slot, my_rows, 0), (1, ROWS, D))[0]
    held = held.reshape(ROWS, NZ, COLS).transpose(1, 0, 2)
    previous = lax.all_to_all(held, Z, 0, 0, tiled=True)
    previous = lax.dynamic_index_in_dim(previous, my_owner, 0, keepdims=False)

    outgoing = grad_partial[0].reshape(NC, NX, 2, RG, ROWS, COLS)
    outgoing = outgoing.transpose(2, 3, 1, 0, 4, 5).reshape(NY * NX * NC, ROWS, COLS)
    arrived = lax.all_to_all(outgoing, DP, 0, 0, tiled=True)
    summed = jnp.sum(arrived.astype(jnp.float32), axis=0).astype(jnp.bfloat16)
    initial = INIT_S * summed.astype(jnp.float32) + INIT_M * previous

    block = spread(initial.astype(jnp.bfloat16), Z, NZ)
    block = spread(block, "y", NY)
    block = spread(block, "x", NX)
    block = block.reshape(HALF, RG, NZ, ROWS, COLS)

    hits = (owners[None, :] == own_index) & (
        slots[None, :] == jnp.arange(DEPTH, dtype=jnp.int32)[:, None]
    )
    present = jnp.sum(hits.astype(jnp.int32), axis=1)
    which = jnp.sum(hits.astype(jnp.int32) * layers[None, :], axis=1) - first
    in_half = (which >= 0) & (which < HALF) & (present > 0)
    near = jnp.take(block, jnp.clip(which, 0, HALF - 1), axis=0)
    near = jnp.where(in_half[:, None, None, None, None], near, jnp.zeros_like(near))
    far = lax.ppermute(near, "core", [(0, 1), (1, 0)])
    momentum_out = update_momentum(present, near, far, momentum[0])[None]

    updated = update_weights(block, weights_half)
    weights_out = lax.all_to_all(updated, "core", 0, 0, tiled=True).reshape(L, E, D)
    return (weights_out, momentum_out)


def solution(mesh):
    mesh = Mesh(mesh.devices.reshape(NY, NX, NC, NZ), ("y", "x", "core", "fsdp"))
    in_specs = (
        P(DP, None, None, Z),
        P(None, None, Z),
        P(Z, None, None, None),
        P(),
    )
    out_specs = (P(), P(Z, None, None, None))
    return jax.shard_map(local, mesh=mesh, in_specs=in_specs, out_specs=out_specs, check_vma=False)
```

```python
import jax
import jax.numpy as jnp
from jax import lax
from jax.experimental import pallas as pl
from jax.experimental.pallas import tpu as pltpu
from jax.sharding import Mesh, PartitionSpec as P

E = 64
D = 2048
L = 16
DEPTH = 4
ITERS = 5
NY, NX, NC, NZ = 8, 4, 2, 16
HALF = L // NC
RG = 4
ROWS = E // RG
COLS = D // NZ
GROUP = 4 * E
DP = ("y", "x", "core")
Z = "fsdp"

coef_a = 3.4445
coef_b = -4.775
coef_c = 2.0315
moment_rate = 0.95
learn_rate = 0.1
decay_rate = 0.1
scale = 0.2 * D**0.5
INIT_S = 1.0 + moment_rate
INIT_M = moment_rate * moment_rate
BACK_I = 1.0 / INIT_S
BACK_M = moment_rate - INIT_M / INIT_S


def ortho_kernel(core_ref, x_ref, w_ref, half_ref, full_ref, xs, ws, w_sem, out_sem):
    fetch = pltpu.make_async_copy(w_ref, ws, w_sem)
    fetch.start()
    for l in range(HALF):
        for z in range(NZ):
            xs[l * E : (l + 1) * E, z * COLS : (z + 1) * COLS] = x_ref[l, :, z].reshape(E, COLS)
    row = lax.broadcasted_iota(jnp.int32, (GROUP, GROUP), 0)
    col = lax.broadcasted_iota(jnp.int32, (GROUP, GROUP), 1)
    same = (row >> 6) == (col >> 6)
    diagonal = row == col
    eye_a = jnp.where(diagonal, coef_a, 0.0)

    def split(a):
        high = a.astype(jnp.bfloat16)
        return high, (a - high.astype(jnp.float32)).astype(jnp.bfloat16)

    def dot(a, b):
        return jnp.dot(a, b, preferred_element_type=jnp.float32)

    def mm(a, b):
        return dot(a[0], b[0]) + (dot(a[0], b[1]) + dot(a[1], b[0]))

    groups = range(HALF * E // GROUP)
    grams, scales = [], []
    for g in groups:
        x = xs[g * GROUP : (g + 1) * GROUP, :]
        gram = lax.dot_general(
            x, x, (((1,), (1,)), ((), ())), preferred_element_type=jnp.float32
        )
        trace = jnp.where(diagonal, gram, 0.0)
        by_row = jnp.sum(trace, axis=1, keepdims=True)
        by_col = jnp.sum(trace, axis=0, keepdims=True)
        total_row = jnp.sum(jnp.where(same, by_col, 0.0), axis=1, keepdims=True)
        total_col = jnp.sum(jnp.where(same, by_row, 0.0), axis=0, keepdims=True)
        inv_row = 1.0 / (jnp.sqrt(total_row) + 1e-07)
        inv_col = 1.0 / (jnp.sqrt(total_col) + 1e-07)
        grams.append(jnp.where(same, gram * inv_row * inv_col, 0.0))
        scales.append(inv_col)
    polys = [None for _ in groups]
    for repeat in range(ITERS):
        gram_parts = [split(gram) for gram in grams]
        squares = [mm(gram, gram) for gram in gram_parts]
        steps = [eye_a + coef_b * gram + coef_c * sq for gram, sq in zip(grams, squares)]
        step_parts = [split(step) for step in steps]
        if repeat < ITERS - 1:
            halfway = [split(mm(step, gram)) for step, gram in zip(step_parts, gram_parts)]
            grams = [mm(half, step) for half, step in zip(halfway, step_parts)]
        polys = [
            step if poly is None else mm(part, split(poly))
            for step, part, poly in zip(steps, step_parts, polys)
        ]
    fetch.wait()
    base = core_ref[0] * HALF
    stores = []
    for g in groups:
        high, low = split(polys[g] * scales[g])
        for z in range(NZ // 2):
            x = xs[g * GROUP : (g + 1) * GROUP, 2 * z * COLS : 2 * (z + 1) * COLS]
            ortho = dot(high, x) + dot(low, x)
            for part in range(2):
                k = 2 * z + part
                wide = ws[k, 4 * g : 4 * (g + 1)].reshape(GROUP, COLS).astype(jnp.float32)
                mine = ortho[:, part * COLS : (part + 1) * COLS]
                new = wide - learn_rate * (scale * mine + decay_rate * wide)
                half_ref[4 * g : 4 * (g + 1), :, k * COLS : (k + 1) * COLS] = new.astype(
                    jnp.bfloat16
                ).reshape(4, E, COLS)
        store = pltpu.make_async_copy(
            half_ref.at[pl.ds(4 * g, 4)], full_ref.at[pl.ds(base + 4 * g, 4)], out_sem.at[g]
        )
        store.start()
        stores.append(store)
    for store in stores:
        store.wait()


def update_weights(core, x, weights):
    return pl.pallas_call(
        ortho_kernel,
        out_shape=(
            jax.ShapeDtypeStruct((HALF, E, D), jnp.bfloat16),
            jax.ShapeDtypeStruct((L, E, D), jnp.bfloat16),
        ),
        in_specs=[
            pl.BlockSpec(memory_space=pltpu.SMEM),
            pl.BlockSpec(memory_space=pltpu.VMEM),
            pl.BlockSpec(memory_space=pltpu.HBM),
        ],
        out_specs=(pl.BlockSpec(memory_space=pltpu.VMEM), pl.BlockSpec(memory_space=pltpu.HBM)),
        scratch_shapes=[
            pltpu.VMEM((HALF * E, D), jnp.bfloat16),
            pltpu.VMEM((NZ, HALF, E, COLS), jnp.bfloat16),
            pltpu.SemaphoreType.DMA(()),
            pltpu.SemaphoreType.DMA((2,)),
        ],
        compiler_params=pltpu.CompilerParams(vmem_limit_bytes=40 * 2**20),
        cost_estimate=pl.CostEstimate(
            flops=10**10, bytes_accessed=8 * 2**20, transcendentals=0
        ),
        name="update_weights",
    )(core, x, weights)


def join_kernel(core_ref, other_ref, mine_ref, full_ref, sem):
    del mine_ref
    base = (NC - 1 - core_ref[0]) * HALF
    copies = [
        pltpu.make_async_copy(
            other_ref.at[pl.ds(2 * k, 2)], full_ref.at[pl.ds(base + 2 * k, 2)], sem.at[k]
        )
        for k in range(HALF // 2)
    ]
    for copy in copies:
        copy.start()
    for copy in copies:
        copy.wait()


def join_halves(core, other, full):
    return pl.pallas_call(
        join_kernel,
        out_shape=jax.ShapeDtypeStruct((L, E, D), jnp.bfloat16),
        in_specs=[
            pl.BlockSpec(memory_space=pltpu.SMEM),
            pl.BlockSpec(memory_space=pl.ANY),
            pl.BlockSpec(memory_space=pl.ANY),
        ],
        out_specs=pl.BlockSpec(memory_space=pl.ANY),
        input_output_aliases={2: 0},
        scratch_shapes=[pltpu.SemaphoreType.DMA((HALF // 2,))],
        name="join_halves",
    )(core, other, full)


def moment_kernel(source_ref, near_ref, far_ref, m_ref, o_ref):
    source = source_ref[pl.program_id(0)]
    for z in range(NZ):
        columns = pl.ds(z * COLS, COLS)
        near = near_ref[0, :, z].astype(jnp.float32)
        far = far_ref[0, :, z].astype(jnp.float32)
        initial = jnp.where(source == 1, near, far).reshape(E, COLS)
        moment = BACK_I * initial + BACK_M * m_ref[0, :, columns]
        o_ref[0, :, columns] = jnp.where(source > 0, moment, 0.0)


def update_momentum(source, near, far, momentum):
    picked = pl.BlockSpec((1, RG, NZ, ROWS, COLS), lambda s, p: (s, 0, 0, 0, 0))
    whole = pl.BlockSpec((1, E, D), lambda s, p: (s, 0, 0))
    return pl.pallas_call(
        moment_kernel,
        out_shape=jax.ShapeDtypeStruct((DEPTH, E, D), jnp.float32),
        grid_spec=pltpu.PrefetchScalarGridSpec(
            num_scalar_prefetch=1,
            grid=(DEPTH,),
            in_specs=[picked, picked, whole],
            out_specs=whole,
        ),
        cost_estimate=pl.CostEstimate(
            flops=4 * 10**6, bytes_accessed=6 * 2**20, transcendentals=0
        ),
        name="update_momentum",
    )(source, near, far, momentum)


def spread(x, axis, count):
    return lax.all_to_all(jnp.broadcast_to(x[None], (count,) + x.shape), axis, 0, 0, tiled=True)


def local(grad_partial, weights, momentum, owners):
    y, x, core = lax.axis_index("y"), lax.axis_index("x"), lax.axis_index("core")
    own_index = lax.axis_index(Z)
    layers = jnp.arange(L, dtype=jnp.int32)
    first = HALF * core
    slots = jnp.sum(
        ((owners[None, :] == owners[:, None]) & (layers[None, :] < layers[:, None])).astype(
            jnp.int32
        ),
        axis=1,
    )

    kept = lax.dynamic_slice_in_dim(weights, first, HALF, 0)
    weights_half = lax.all_gather(kept, Z)

    my_layer = first + 2 * x + y // RG
    my_rows = (y % RG) * ROWS
    my_owner = lax.dynamic_index_in_dim(owners, my_layer, 0, keepdims=False)
    my_slot = lax.dynamic_index_in_dim(slots, my_layer, 0, keepdims=False)

    held = lax.dynamic_slice(momentum[0], (my_slot, my_rows, 0), (1, ROWS, D))[0]
    held = held.astype(jnp.bfloat16).reshape(ROWS, NZ, COLS).transpose(1, 0, 2)
    previous = lax.all_to_all(held, Z, 0, 0, tiled=True)
    previous = lax.dynamic_index_in_dim(previous, my_owner, 0, keepdims=False).astype(jnp.float32)

    outgoing = grad_partial[0].reshape(L * RG, ROWS, COLS)
    arrived = lax.all_to_all(outgoing, ("core", "x", "y"), 0, 0, tiled=True)
    summed = jnp.sum(arrived.astype(jnp.float32), axis=0)
    initial = INIT_S * summed + INIT_M * previous

    block = spread(initial.astype(jnp.bfloat16), Z, NZ)
    block = spread(block, "y", NY)
    block = spread(block, "x", NX)
    block = block.reshape(HALF, RG, NZ, ROWS, COLS)

    hits = (owners[None, :] == own_index) & (
        slots[None, :] == jnp.arange(DEPTH, dtype=jnp.int32)[:, None]
    )
    present = jnp.sum(hits.astype(jnp.int32), axis=1)
    which = jnp.sum(hits.astype(jnp.int32) * layers[None, :], axis=1)
    in_half = (which >= first) & (which < first + HALF)
    source = jnp.where(present > 0, jnp.where(in_half, 1, 2), 0).astype(jnp.int32)
    near = jnp.take(block, which % HALF, axis=0, mode="clip")
    far = lax.ppermute(near, "core", [(0, 1), (1, 0)])

    where = core.astype(jnp.int32)[None]
    block, near = lax.optimization_barrier((block, near))
    half, full = update_weights(where, block, weights_half)
    other = lax.ppermute(half, "core", [(0, 1), (1, 0)])
    momentum_out = update_momentum(source, near, far, momentum[0])[None]
    weights_out = join_halves(where, other, full)
    return (weights_out, momentum_out)


def solution(mesh):
    mesh = Mesh(mesh.devices.reshape(NY, NX, NC, NZ), ("y", "x", "core", "fsdp"))
    in_specs = (
        P(DP, None, None, Z),
        P(None, None, Z),
        P(Z, None, None, None),
        P(),
    )
    out_specs = (P(), P(Z, None, None, None))
    return jax.shard_map(local, mesh=mesh, in_specs=in_specs, out_specs=out_specs, check_vma=False)
```

```python
import jax
import jax.numpy as jnp
from jax import lax
from jax.experimental import pallas as pl
from jax.experimental.pallas import tpu as pltpu
from jax.sharding import Mesh, PartitionSpec as P

E = 64
D = 2048
L = 16
DEPTH = 4
ITERS = 5
NY, NX, NC, NZ = 8, 4, 2, 16
HALF = L // NC
RG = 4
ROWS = E // RG
COLS = D // NZ
GROUP = 4 * E
DP = ("y", "x", "core")
Z = "fsdp"

coef_a = 3.4445
coef_b = -4.775
coef_c = 2.0315
moment_rate = 0.95
learn_rate = 0.1
decay_rate = 0.1
scale = 0.2 * D**0.5
INIT_S = 1.0 + moment_rate
INIT_M = moment_rate * moment_rate
BACK_I = 1.0 / INIT_S
BACK_M = moment_rate - INIT_M / INIT_S


def split(a):
    high = a.astype(jnp.bfloat16)
    return high, (a - high.astype(jnp.float32)).astype(jnp.bfloat16)


def dot(a, b):
    return jnp.dot(a, b, preferred_element_type=jnp.float32)


def poly_kernel(x_ref, xs, high_ref, low_ref):
    for l in range(HALF):
        for z in range(NZ):
            xs[l * E : (l + 1) * E, z * COLS : (z + 1) * COLS] = x_ref[l, :, z].reshape(E, COLS)
    row = lax.broadcasted_iota(jnp.int32, (GROUP, GROUP), 0)
    col = lax.broadcasted_iota(jnp.int32, (GROUP, GROUP), 1)
    same = (row >> 6) == (col >> 6)
    diagonal = row == col
    eye_a = jnp.where(diagonal, coef_a, 0.0)

    def mm(a, b):
        return dot(a[0], b[0]) + (dot(a[0], b[1]) + dot(a[1], b[0]))

    groups = range(HALF * E // GROUP)
    grams, scales = [], []
    for g in groups:
        x = xs[g * GROUP : (g + 1) * GROUP, :]
        gram = lax.dot_general(
            x, x, (((1,), (1,)), ((), ())), preferred_element_type=jnp.float32
        )
        trace = jnp.where(diagonal, gram, 0.0)
        by_row = jnp.sum(trace, axis=1, keepdims=True)
        by_col = jnp.sum(trace, axis=0, keepdims=True)
        total_row = jnp.sum(jnp.where(same, by_col, 0.0), axis=1, keepdims=True)
        total_col = jnp.sum(jnp.where(same, by_row, 0.0), axis=0, keepdims=True)
        inv_row = 1.0 / (jnp.sqrt(total_row) + 1e-07)
        inv_col = 1.0 / (jnp.sqrt(total_col) + 1e-07)
        grams.append(jnp.where(same, gram * inv_row * inv_col, 0.0))
        scales.append(inv_col)
    polys = [None for _ in groups]
    for repeat in range(ITERS):
        gram_parts = [split(gram) for gram in grams]
        squares = [mm(gram, gram) for gram in gram_parts]
        steps = [eye_a + coef_b * gram + coef_c * sq for gram, sq in zip(grams, squares)]
        step_parts = [split(step) for step in steps]
        if repeat < ITERS - 1:
            halfway = [split(mm(step, gram)) for step, gram in zip(step_parts, gram_parts)]
            grams = [mm(half, step) for half, step in zip(halfway, step_parts)]
        polys = [
            step if poly is None else mm(part, split(poly))
            for step, part, poly in zip(steps, step_parts, polys)
        ]
    for g in groups:
        high_ref[g], low_ref[g] = split(polys[g] * scales[g])


def polynomials(x):
    vmem = pl.BlockSpec(memory_space=pltpu.VMEM)
    poly = jax.ShapeDtypeStruct((HALF * E // GROUP, GROUP, GROUP), jnp.bfloat16)
    return pl.pallas_call(
        poly_kernel,
        out_shape=(jax.ShapeDtypeStruct((HALF * E, D), jnp.bfloat16), poly, poly),
        in_specs=[vmem],
        out_specs=(vmem, vmem, vmem),
        compiler_params=pltpu.CompilerParams(vmem_limit_bytes=24 * 2**20),
        cost_estimate=pl.CostEstimate(
            flops=8 * 10**9, bytes_accessed=4 * 2**20, transcendentals=0
        ),
        name="polynomials",
    )(x)


def weights_kernel(core_ref, xs, high_ref, low_ref, w_ref, half_ref, full_ref, out_sem):
    base = core_ref[0] * HALF
    stores = []
    for g in range(HALF * E // GROUP):
        high, low = high_ref[g], low_ref[g]
        for z in range(NZ // 2):
            x = xs[g * GROUP : (g + 1) * GROUP, 2 * z * COLS : 2 * (z + 1) * COLS]
            ortho = dot(high, x) + dot(low, x)
            for part in range(2):
                k = 2 * z + part
                wide = w_ref[k, 4 * g : 4 * (g + 1)].reshape(GROUP, COLS).astype(jnp.float32)
                mine = ortho[:, part * COLS : (part + 1) * COLS]
                new = wide - learn_rate * (scale * mine + decay_rate * wide)
                half_ref[4 * g : 4 * (g + 1), :, k * COLS : (k + 1) * COLS] = new.astype(
                    jnp.bfloat16
                ).reshape(4, E, COLS)
        store = pltpu.make_async_copy(
            half_ref.at[pl.ds(4 * g, 4)], full_ref.at[pl.ds(base + 4 * g, 4)], out_sem.at[g]
        )
        store.start()
        stores.append(store)
    for store in stores:
        store.wait()


def update_weights(core, xs, high, low, weights):
    vmem = pl.BlockSpec(memory_space=pltpu.VMEM)
    return pl.pallas_call(
        weights_kernel,
        out_shape=(
            jax.ShapeDtypeStruct((HALF, E, D), jnp.bfloat16),
            jax.ShapeDtypeStruct((L, E, D), jnp.bfloat16),
        ),
        in_specs=[pl.BlockSpec(memory_space=pltpu.SMEM), vmem, vmem, vmem, vmem],
        out_specs=(vmem, pl.BlockSpec(memory_space=pltpu.HBM)),
        scratch_shapes=[pltpu.SemaphoreType.DMA((2,))],
        compiler_params=pltpu.CompilerParams(vmem_limit_bytes=24 * 2**20),
        cost_estimate=pl.CostEstimate(
            flops=2 * 10**9, bytes_accessed=8 * 2**20, transcendentals=0
        ),
        name="update_weights",
    )(core, xs, high, low, weights)


def finish_kernel(
    core_ref, source_ref, other_ref, near_ref, far_ref, m_ref, mine_ref, full_ref, o_ref, ms, sem, m_sem
):
    del mine_ref
    base = (NC - 1 - core_ref[0]) * HALF
    copies = [
        pltpu.make_async_copy(
            other_ref.at[pl.ds(2 * k, 2)], full_ref.at[pl.ds(base + 2 * k, 2)], sem.at[k]
        )
        for k in range(HALF // 2)
    ]
    for copy in copies:
        copy.start()
    for s in range(DEPTH):
        source = source_ref[s]
        for z in range(NZ):
            columns = slice(z * COLS, (z + 1) * COLS)
            near = near_ref[s, :, z].astype(jnp.float32)
            far = far_ref[s, :, z].astype(jnp.float32)
            initial = jnp.where(source == 1, near, far).reshape(E, COLS)
            moment = BACK_I * initial + BACK_M * m_ref[s, :, columns]
            ms[s, :, columns] = jnp.where(source > 0, moment, 0.0)
        copy = pltpu.make_async_copy(ms.at[s], o_ref.at[s], m_sem.at[s])
        copy.start()
        copies.append(copy)
    for copy in copies:
        copy.wait()


def finish(core, source, other, near, far, momentum, full):
    smem = pl.BlockSpec(memory_space=pltpu.SMEM)
    vmem = pl.BlockSpec(memory_space=pltpu.VMEM)
    hbm = pl.BlockSpec(memory_space=pltpu.HBM)
    return pl.pallas_call(
        finish_kernel,
        out_shape=(
            jax.ShapeDtypeStruct((L, E, D), jnp.bfloat16),
            jax.ShapeDtypeStruct((DEPTH, E, D), jnp.float32),
        ),
        in_specs=[smem, smem, vmem, vmem, vmem, vmem, hbm],
        out_specs=(hbm, hbm),
        input_output_aliases={6: 0},
        scratch_shapes=[
            pltpu.VMEM((DEPTH, E, D), jnp.float32),
            pltpu.SemaphoreType.DMA((HALF // 2,)),
            pltpu.SemaphoreType.DMA((DEPTH,)),
        ],
        compiler_params=pltpu.CompilerParams(vmem_limit_bytes=32 * 2**20),
        cost_estimate=pl.CostEstimate(
            flops=4 * 10**6, bytes_accessed=10 * 2**20, transcendentals=0
        ),
        name="finish",
    )(core, source, other, near, far, momentum, full)


def spread(x, axis, count):
    return lax.all_to_all(jnp.broadcast_to(x[None], (count,) + x.shape), axis, 0, 0, tiled=True)


def local(grad_partial, weights, momentum, owners):
    y, x, core = lax.axis_index("y"), lax.axis_index("x"), lax.axis_index("core")
    own_index = lax.axis_index(Z)
    layers = jnp.arange(L, dtype=jnp.int32)
    first = HALF * core
    slots = jnp.sum(
        ((owners[None, :] == owners[:, None]) & (layers[None, :] < layers[:, None])).astype(
            jnp.int32
        ),
        axis=1,
    )

    kept = lax.dynamic_slice_in_dim(weights, first, HALF, 0)
    weights_half = lax.all_gather(kept, Z)

    my_layer = first + 2 * x + y // RG
    my_rows = (y % RG) * ROWS
    my_owner = lax.dynamic_index_in_dim(owners, my_layer, 0, keepdims=False)
    my_slot = lax.dynamic_index_in_dim(slots, my_layer, 0, keepdims=False)

    held = lax.dynamic_slice(momentum[0], (my_slot, my_rows, 0), (1, ROWS, D))[0]
    held = held.astype(jnp.bfloat16).reshape(ROWS, NZ, COLS).transpose(1, 0, 2)
    previous = lax.all_to_all(held, Z, 0, 0, tiled=True)
    previous = lax.dynamic_index_in_dim(previous, my_owner, 0, keepdims=False).astype(jnp.float32)

    outgoing = grad_partial[0].reshape(L * RG, ROWS, COLS)
    arrived = lax.all_to_all(outgoing, ("core", "x", "y"), 0, 0, tiled=True)
    summed = jnp.sum(arrived.astype(jnp.float32), axis=0)
    initial = INIT_S * summed + INIT_M * previous

    block = spread(initial.astype(jnp.bfloat16), Z, NZ)
    block = spread(block, "y", NY)
    block = spread(block, "x", NX)
    block = block.reshape(HALF, RG, NZ, ROWS, COLS)

    hits = (owners[None, :] == own_index) & (
        slots[None, :] == jnp.arange(DEPTH, dtype=jnp.int32)[:, None]
    )
    present = jnp.sum(hits.astype(jnp.int32), axis=1)
    which = jnp.sum(hits.astype(jnp.int32) * layers[None, :], axis=1)
    in_half = (which >= first) & (which < first + HALF)
    source = jnp.where(present > 0, jnp.where(in_half, 1, 2), 0).astype(jnp.int32)
    near = jnp.take(block, which % HALF, axis=0, mode="clip")

    where = core.astype(jnp.int32)[None]
    block, near, weights_half = lax.optimization_barrier((block, near, weights_half))
    far = lax.ppermute(near, "core", [(0, 1), (1, 0)])
    xs, high, low = polynomials(block)
    xs, high, low, far = lax.optimization_barrier((xs, high, low, far))
    half, full = update_weights(where, xs, high, low, weights_half)
    other = lax.ppermute(half, "core", [(0, 1), (1, 0)])
    weights_out, moment = finish(where, source, other, near, far, momentum[0], full)
    return (weights_out, moment[None])


def solution(mesh):
    mesh = Mesh(mesh.devices.reshape(NY, NX, NC, NZ), ("y", "x", "core", "fsdp"))
    in_specs = (
        P(DP, None, None, Z),
        P(None, None, Z),
        P(Z, None, None, None),
        P(),
    )
    out_specs = (P(), P(Z, None, None, None))
    return jax.shard_map(local, mesh=mesh, in_specs=in_specs, out_specs=out_specs, check_vma=False)
```

```python
import jax
import jax.numpy as jnp
from jax import lax
from jax.experimental import pallas as pl
from jax.experimental.pallas import tpu as pltpu
from jax.sharding import Mesh, PartitionSpec as P

E = 64
D = 2048
L = 16
DEPTH = 4
ITERS = 5
NY, NX, NC, NZ = 8, 4, 2, 16
HALF = L // NC
RG = 4
ROWS = E // RG
COLS = D // NZ
GROUP = 4 * E
DP = ("y", "x", "core")
Z = "fsdp"

coef_a = 3.4445
coef_b = -4.775
coef_c = 2.0315
moment_rate = 0.95
learn_rate = 0.1
decay_rate = 0.1
scale = 0.2 * D**0.5
INIT_S = 1.0 + moment_rate
INIT_M = moment_rate * moment_rate
BACK_I = 1.0 / INIT_S
BACK_M = moment_rate - INIT_M / INIT_S


def split(a):
    high = a.astype(jnp.bfloat16)
    return high, (a - high.astype(jnp.float32)).astype(jnp.bfloat16)


def dot(a, b):
    return jnp.dot(a, b, preferred_element_type=jnp.float32)


def assemble_kernel(index_ref, own_ref, left_ref, right_ref, far0_ref, far1_ref, xs, near_ref):
    pieces = [
        (own_ref, 0, 0, 0),
        (own_ref, RG, 0, 1),
        (left_ref, 0, 1, 0),
        (left_ref, RG, 1, 1),
        (far0_ref, 0, 2, 0),
        (far1_ref, 0, 2, 1),
        (right_ref, 0, 3, 0),
        (right_ref, RG, 3, 1),
    ]
    for ref, at, place, part in pieces:
        layer = 2 * index_ref[place] + part
        for z in range(NZ):
            xs[layer, :, z * COLS : (z + 1) * COLS] = ref[at : at + RG, z].reshape(E, COLS)
    for s in range(DEPTH):
        near_ref[s] = xs[index_ref[NX + s]]


def assemble(index, own, left, right, far0, far1):
    vmem = pl.BlockSpec(memory_space=pltpu.VMEM)
    return pl.pallas_call(
        assemble_kernel,
        out_shape=(
            jax.ShapeDtypeStruct((HALF, E, D), jnp.bfloat16),
            jax.ShapeDtypeStruct((DEPTH, E, D), jnp.bfloat16),
        ),
        in_specs=[pl.BlockSpec(memory_space=pltpu.SMEM)] + [vmem] * 5,
        out_specs=(vmem, vmem),
        compiler_params=pltpu.CompilerParams(vmem_limit_bytes=16 * 2**20),
        cost_estimate=pl.CostEstimate(flops=0, bytes_accessed=4 * 2**20, transcendentals=0),
        name="assemble",
    )(index, own, left, right, far0, far1)


def poly_kernel(xs, high_ref, low_ref):
    row = lax.broadcasted_iota(jnp.int32, (GROUP, GROUP), 0)
    col = lax.broadcasted_iota(jnp.int32, (GROUP, GROUP), 1)
    same = (row >> 6) == (col >> 6)
    diagonal = row == col
    eye_a = jnp.where(diagonal, coef_a, 0.0)

    def mm(a, b):
        return dot(a[0], b[0]) + (dot(a[0], b[1]) + dot(a[1], b[0]))

    groups = range(HALF * E // GROUP)
    grams, scales = [], []
    for g in groups:
        x = xs[g * GROUP : (g + 1) * GROUP, :]
        gram = lax.dot_general(
            x, x, (((1,), (1,)), ((), ())), preferred_element_type=jnp.float32
        )
        trace = jnp.where(diagonal, gram, 0.0)
        by_row = jnp.sum(trace, axis=1, keepdims=True)
        by_col = jnp.sum(trace, axis=0, keepdims=True)
        total_row = jnp.sum(jnp.where(same, by_col, 0.0), axis=1, keepdims=True)
        total_col = jnp.sum(jnp.where(same, by_row, 0.0), axis=0, keepdims=True)
        inv_row = 1.0 / (jnp.sqrt(total_row) + 1e-07)
        inv_col = 1.0 / (jnp.sqrt(total_col) + 1e-07)
        grams.append(jnp.where(same, gram * inv_row * inv_col, 0.0))
        scales.append(inv_col)
    polys = [None for _ in groups]
    for repeat in range(ITERS):
        gram_parts = [split(gram) for gram in grams]
        squares = [mm(gram, gram) for gram in gram_parts]
        steps = [eye_a + coef_b * gram + coef_c * sq for gram, sq in zip(grams, squares)]
        step_parts = [split(step) for step in steps]
        if repeat < ITERS - 1:
            halfway = [split(mm(step, gram)) for step, gram in zip(step_parts, gram_parts)]
            grams = [mm(half, step) for half, step in zip(halfway, step_parts)]
        polys = [
            step if poly is None else mm(part, split(poly))
            for step, part, poly in zip(steps, step_parts, polys)
        ]
    for g in groups:
        high_ref[g], low_ref[g] = split(polys[g] * scales[g])


def polynomials(x):
    vmem = pl.BlockSpec(memory_space=pltpu.VMEM)
    poly = jax.ShapeDtypeStruct((HALF * E // GROUP, GROUP, GROUP), jnp.bfloat16)
    return pl.pallas_call(
        poly_kernel,
        out_shape=(poly, poly),
        in_specs=[vmem],
        out_specs=(vmem, vmem),
        compiler_params=pltpu.CompilerParams(vmem_limit_bytes=16 * 2**20),
        cost_estimate=pl.CostEstimate(
            flops=8 * 10**9, bytes_accessed=4 * 2**20, transcendentals=0
        ),
        name="polynomials",
    )(x)


def weights_kernel(core_ref, xs, high_ref, low_ref, w_ref, half_ref, full_ref, out_sem):
    base = core_ref[0] * HALF
    stores = []
    for g in range(HALF * E // GROUP):
        high, low = high_ref[g], low_ref[g]
        for z in range(NZ // 2):
            x = xs[g * GROUP : (g + 1) * GROUP, 2 * z * COLS : 2 * (z + 1) * COLS]
            ortho = dot(high, x) + dot(low, x)
            for part in range(2):
                k = 2 * z + part
                wide = w_ref[k, 4 * g : 4 * (g + 1)].reshape(GROUP, COLS).astype(jnp.float32)
                mine = ortho[:, part * COLS : (part + 1) * COLS]
                new = wide - learn_rate * (scale * mine + decay_rate * wide)
                half_ref[4 * g : 4 * (g + 1), :, k * COLS : (k + 1) * COLS] = new.astype(
                    jnp.bfloat16
                ).reshape(4, E, COLS)
        store = pltpu.make_async_copy(
            half_ref.at[pl.ds(4 * g, 4)], full_ref.at[pl.ds(base + 4 * g, 4)], out_sem.at[g]
        )
        store.start()
        stores.append(store)
    for store in stores:
        store.wait()


def update_weights(core, xs, high, low, weights):
    vmem = pl.BlockSpec(memory_space=pltpu.VMEM)
    return pl.pallas_call(
        weights_kernel,
        out_shape=(
            jax.ShapeDtypeStruct((HALF, E, D), jnp.bfloat16),
            jax.ShapeDtypeStruct((L, E, D), jnp.bfloat16),
        ),
        in_specs=[pl.BlockSpec(memory_space=pltpu.SMEM), vmem, vmem, vmem, vmem],
        out_specs=(vmem, pl.BlockSpec(memory_space=pltpu.HBM)),
        scratch_shapes=[pltpu.SemaphoreType.DMA((2,))],
        compiler_params=pltpu.CompilerParams(vmem_limit_bytes=16 * 2**20),
        cost_estimate=pl.CostEstimate(
            flops=2 * 10**9, bytes_accessed=8 * 2**20, transcendentals=0
        ),
        name="update_weights",
    )(core, xs, high, low, weights)


def join_kernel(core_ref, other_ref, mine_ref, full_ref, sem):
    del mine_ref
    base = (NC - 1 - core_ref[0]) * HALF
    copies = [
        pltpu.make_async_copy(
            other_ref.at[pl.ds(2 * k, 2)], full_ref.at[pl.ds(base + 2 * k, 2)], sem.at[k]
        )
        for k in range(HALF // 2)
    ]
    for copy in copies:
        copy.start()
    for copy in copies:
        copy.wait()


def join_halves(core, other, full):
    hbm = pl.BlockSpec(memory_space=pltpu.HBM)
    return pl.pallas_call(
        join_kernel,
        out_shape=jax.ShapeDtypeStruct((L, E, D), jnp.bfloat16),
        in_specs=[
            pl.BlockSpec(memory_space=pltpu.SMEM),
            pl.BlockSpec(memory_space=pltpu.VMEM),
            hbm,
        ],
        out_specs=hbm,
        input_output_aliases={2: 0},
        scratch_shapes=[pltpu.SemaphoreType.DMA((HALF // 2,))],
        compiler_params=pltpu.CompilerParams(vmem_limit_bytes=8 * 2**20),
        name="join_halves",
    )(core, other, full)


def moment_kernel(source_ref, near_ref, far_ref, m_ref, o_ref, ms, sem):
    copies = []
    for s in range(DEPTH):
        source = source_ref[s]
        for z in range(NZ):
            columns = slice(z * COLS, (z + 1) * COLS)
            near = near_ref[s, :, columns].astype(jnp.float32)
            far = far_ref[s, :, columns].astype(jnp.float32)
            initial = jnp.where(source == 1, near, far)
            moment = BACK_I * initial + BACK_M * m_ref[s, :, columns]
            ms[s, :, columns] = jnp.where(source > 0, moment, 0.0)
        copy = pltpu.make_async_copy(ms.at[s], o_ref.at[s], sem.at[s])
        copy.start()
        copies.append(copy)
    for copy in copies:
        copy.wait()


def update_momentum(source, near, far, momentum):
    vmem = pl.BlockSpec(memory_space=pltpu.VMEM)
    return pl.pallas_call(
        moment_kernel,
        out_shape=jax.ShapeDtypeStruct((DEPTH, E, D), jnp.float32),
        in_specs=[pl.BlockSpec(memory_space=pltpu.SMEM), vmem, vmem, vmem],
        out_specs=pl.BlockSpec(memory_space=pltpu.HBM),
        scratch_shapes=[
            pltpu.VMEM((DEPTH, E, D), jnp.float32),
            pltpu.SemaphoreType.DMA((DEPTH,)),
        ],
        compiler_params=pltpu.CompilerParams(vmem_limit_bytes=16 * 2**20),
        cost_estimate=pl.CostEstimate(
            flops=4 * 10**6, bytes_accessed=6 * 2**20, transcendentals=0
        ),
        name="update_momentum",
    )(source, near, far, momentum)


def spread(x, axis, count):
    return lax.all_to_all(jnp.broadcast_to(x[None], (count,) + x.shape), axis, 0, 0, tiled=True)


def local(grad_partial, weights, momentum, owners):
    y, x, core = lax.axis_index("y"), lax.axis_index("x"), lax.axis_index("core")
    own_index = lax.axis_index(Z)
    layers = jnp.arange(L, dtype=jnp.int32)
    first = HALF * core
    slots = jnp.sum(
        ((owners[None, :] == owners[:, None]) & (layers[None, :] < layers[:, None])).astype(
            jnp.int32
        ),
        axis=1,
    )

    kept = lax.dynamic_slice_in_dim(weights, first, HALF, 0)
    weights_half = lax.all_gather(kept, Z)

    my_layer = first + 2 * x + y // RG
    my_rows = (y % RG) * ROWS
    my_owner = lax.dynamic_index_in_dim(owners, my_layer, 0, keepdims=False)
    my_slot = lax.dynamic_index_in_dim(slots, my_layer, 0, keepdims=False)

    held = lax.dynamic_slice(momentum[0], (my_slot, my_rows, 0), (1, ROWS, D))[0]
    held = held.astype(jnp.bfloat16).reshape(ROWS, NZ, COLS).transpose(1, 0, 2)
    previous = lax.all_to_all(held, Z, 0, 0, tiled=True)
    previous = lax.dynamic_index_in_dim(previous, my_owner, 0, keepdims=False).astype(jnp.float32)

    outgoing = grad_partial[0].reshape(L * RG, ROWS, COLS)
    arrived = lax.all_to_all(outgoing, ("core", "x", "y"), 0, 0, tiled=True)
    summed = jnp.sum(arrived.astype(jnp.float32), axis=0)
    initial = INIT_S * summed + INIT_M * previous

    block = spread(initial.astype(jnp.bfloat16), Z, NZ)
    block = spread(block, "y", NY)
    ahead = [(k, (k + 1) % NX) for k in range(NX)]
    back = [(k, (k - 1) % NX) for k in range(NX)]
    left = lax.ppermute(block, "x", ahead)
    right = lax.ppermute(block, "x", back)
    far0 = lax.ppermute(left[:RG], "x", ahead)
    far1 = lax.ppermute(right[RG:], "x", back)

    hits = (owners[None, :] == own_index) & (
        slots[None, :] == jnp.arange(DEPTH, dtype=jnp.int32)[:, None]
    )
    present = jnp.sum(hits.astype(jnp.int32), axis=1)
    which = jnp.sum(hits.astype(jnp.int32) * layers[None, :], axis=1)
    in_half = (which >= first) & (which < first + HALF)
    source = jnp.where(present > 0, jnp.where(in_half, 1, 2), 0).astype(jnp.int32)
    places = (x + jnp.array([0, NX - 1, 2, 1], jnp.int32)) % NX
    index = jnp.concatenate([places, which % HALF]).astype(jnp.int32)
    xs, near = assemble(index, block, left, right, far0, far1)

    where = core.astype(jnp.int32)[None]
    xs, near, weights_half = lax.optimization_barrier((xs, near, weights_half))
    xs = xs.reshape(HALF * E, D)
    far = lax.ppermute(near, "core", [(0, 1), (1, 0)])
    high, low = polynomials(xs)
    high, low, far = lax.optimization_barrier((high, low, far))
    half, full = update_weights(where, xs, high, low, weights_half)
    other = lax.ppermute(half, "core", [(0, 1), (1, 0)])
    moment = update_momentum(source, near, far, momentum[0])
    weights_out = join_halves(where, other, full)
    return (weights_out, moment[None])


def solution(mesh):
    mesh = Mesh(mesh.devices.reshape(NY, NX, NC, NZ), ("y", "x", "core", "fsdp"))
    in_specs = (
        P(DP, None, None, Z),
        P(None, None, Z),
        P(Z, None, None, None),
        P(),
    )
    out_specs = (P(), P(Z, None, None, None))
    return jax.shard_map(local, mesh=mesh, in_specs=in_specs, out_specs=out_specs, check_vma=False)
```

```python
import jax
import jax.numpy as jnp
from jax import lax
from jax.experimental import pallas as pl
from jax.experimental.pallas import tpu as pltpu
from jax.sharding import Mesh, PartitionSpec as P

E = 64
D = 2048
L = 16
DEPTH = 4
ITERS = 5
NY, NX, NC, NZ = 8, 4, 2, 16
HALF = L // NC
RG = 4
ROWS = E // RG
COLS = D // NZ
GROUP = 4 * E
DP = ("y", "x", "core")
Z = "fsdp"

coef_a = 3.4445
coef_b = -4.775
coef_c = 2.0315
moment_rate = 0.95
learn_rate = 0.1
decay_rate = 0.1
scale = 0.2 * D**0.5
INIT_S = 1.0 + moment_rate
INIT_M = moment_rate * moment_rate
BACK_I = 1.0 / INIT_S
BACK_M = moment_rate - INIT_M / INIT_S


def split(a):
    high = a.astype(jnp.bfloat16)
    return high, (a - high.astype(jnp.float32)).astype(jnp.bfloat16)


def dot(a, b):
    return jnp.dot(a, b, preferred_element_type=jnp.float32)


def assemble_kernel(index_ref, own_ref, *refs):
    *pieces, xs, near_ref = refs
    pieces = [(ref, 0, 1 + k // 2, k % 2) for k, ref in enumerate(pieces)]
    pieces += [(own_ref, part * RG, 0, part) for part in range(2)]
    for ref, at, place, part in pieces:
        layer = 2 * index_ref[place] + part
        for z in range(NZ):
            xs[layer, :, z * COLS : (z + 1) * COLS] = ref[at : at + RG, z].reshape(E, COLS)
    for s in range(DEPTH):
        near_ref[s] = xs[index_ref[NX + s]]


def assemble(index, own, *others):
    vmem = pl.BlockSpec(memory_space=pltpu.VMEM)
    return pl.pallas_call(
        assemble_kernel,
        out_shape=(
            jax.ShapeDtypeStruct((HALF, E, D), jnp.bfloat16),
            jax.ShapeDtypeStruct((DEPTH, E, D), jnp.bfloat16),
        ),
        in_specs=[pl.BlockSpec(memory_space=pltpu.SMEM), vmem] + [vmem] * len(others),
        out_specs=(vmem, vmem),
        compiler_params=pltpu.CompilerParams(vmem_limit_bytes=16 * 2**20),
        cost_estimate=pl.CostEstimate(flops=0, bytes_accessed=4 * 2**20, transcendentals=0),
        name="assemble",
    )(index, own, *others)


def poly_kernel(xs, high_ref, low_ref):
    row = lax.broadcasted_iota(jnp.int32, (GROUP, GROUP), 0)
    col = lax.broadcasted_iota(jnp.int32, (GROUP, GROUP), 1)
    same = (row >> 6) == (col >> 6)
    diagonal = row == col
    eye_a = jnp.where(diagonal, coef_a, 0.0)

    def mm(a, b):
        return dot(a[0], b[0]) + (dot(a[0], b[1]) + dot(a[1], b[0]))

    groups = range(HALF * E // GROUP)
    grams, scales = [], []
    for g in groups:
        x = xs[g * GROUP : (g + 1) * GROUP, :]
        gram = lax.dot_general(
            x, x, (((1,), (1,)), ((), ())), preferred_element_type=jnp.float32
        )
        trace = jnp.where(diagonal, gram, 0.0)
        by_row = jnp.sum(trace, axis=1, keepdims=True)
        by_col = jnp.sum(trace, axis=0, keepdims=True)
        total_row = jnp.sum(jnp.where(same, by_col, 0.0), axis=1, keepdims=True)
        total_col = jnp.sum(jnp.where(same, by_row, 0.0), axis=0, keepdims=True)
        inv_row = 1.0 / (jnp.sqrt(total_row) + 1e-07)
        inv_col = 1.0 / (jnp.sqrt(total_col) + 1e-07)
        grams.append(jnp.where(same, gram * inv_row * inv_col, 0.0))
        scales.append(inv_col)
    polys = [None for _ in groups]
    for repeat in range(ITERS):
        gram_parts = [split(gram) for gram in grams]
        squares = [mm(gram, gram) for gram in gram_parts]
        steps = [eye_a + coef_b * gram + coef_c * sq for gram, sq in zip(grams, squares)]
        step_parts = [split(step) for step in steps]
        if repeat < ITERS - 1:
            halfway = [split(mm(step, gram)) for step, gram in zip(step_parts, gram_parts)]
            grams = [mm(half, step) for half, step in zip(halfway, step_parts)]
        polys = [
            step if poly is None else mm(part, split(poly))
            for step, part, poly in zip(steps, step_parts, polys)
        ]
    for g in groups:
        high_ref[g], low_ref[g] = split(polys[g] * scales[g])


def polynomials(x):
    vmem = pl.BlockSpec(memory_space=pltpu.VMEM)
    poly = jax.ShapeDtypeStruct((HALF * E // GROUP, GROUP, GROUP), jnp.bfloat16)
    return pl.pallas_call(
        poly_kernel,
        out_shape=(poly, poly),
        in_specs=[vmem],
        out_specs=(vmem, vmem),
        compiler_params=pltpu.CompilerParams(vmem_limit_bytes=16 * 2**20),
        cost_estimate=pl.CostEstimate(
            flops=8 * 10**9, bytes_accessed=4 * 2**20, transcendentals=0
        ),
        name="polynomials",
    )(x)


def weights_kernel(core_ref, xs, high_ref, low_ref, w_ref, half_ref, full_ref, out_sem):
    base = core_ref[0] * HALF
    stores = []
    for g in range(HALF * E // GROUP):
        high, low = high_ref[g], low_ref[g]
        for z in range(NZ // 2):
            x = xs[g * GROUP : (g + 1) * GROUP, 2 * z * COLS : 2 * (z + 1) * COLS]
            ortho = dot(high, x) + dot(low, x)
            for part in range(2):
                k = 2 * z + part
                wide = w_ref[k, 4 * g : 4 * (g + 1)].reshape(GROUP, COLS).astype(jnp.float32)
                mine = ortho[:, part * COLS : (part + 1) * COLS]
                new = wide - learn_rate * (scale * mine + decay_rate * wide)
                half_ref[4 * g : 4 * (g + 1), :, k * COLS : (k + 1) * COLS] = new.astype(
                    jnp.bfloat16
                ).reshape(4, E, COLS)
        store = pltpu.make_async_copy(
            half_ref.at[pl.ds(4 * g, 4)], full_ref.at[pl.ds(base + 4 * g, 4)], out_sem.at[g]
        )
        store.start()
        stores.append(store)
    for store in stores:
        store.wait()


def update_weights(core, xs, high, low, weights):
    vmem = pl.BlockSpec(memory_space=pltpu.VMEM)
    return pl.pallas_call(
        weights_kernel,
        out_shape=(
            jax.ShapeDtypeStruct((HALF, E, D), jnp.bfloat16),
            jax.ShapeDtypeStruct((L, E, D), jnp.bfloat16),
        ),
        in_specs=[pl.BlockSpec(memory_space=pltpu.SMEM), vmem, vmem, vmem, vmem],
        out_specs=(vmem, pl.BlockSpec(memory_space=pltpu.HBM)),
        scratch_shapes=[pltpu.SemaphoreType.DMA((2,))],
        compiler_params=pltpu.CompilerParams(vmem_limit_bytes=16 * 2**20),
        cost_estimate=pl.CostEstimate(
            flops=2 * 10**9, bytes_accessed=8 * 2**20, transcendentals=0
        ),
        name="update_weights",
    )(core, xs, high, low, weights)


def join_kernel(core_ref, other_ref, mine_ref, full_ref, sem):
    del mine_ref
    base = (NC - 1 - core_ref[0]) * HALF
    copies = [
        pltpu.make_async_copy(
            other_ref.at[pl.ds(2 * k, 2)], full_ref.at[pl.ds(base + 2 * k, 2)], sem.at[k]
        )
        for k in range(HALF // 2)
    ]
    for copy in copies:
        copy.start()
    for copy in copies:
        copy.wait()


def join_halves(core, other, full):
    hbm = pl.BlockSpec(memory_space=pltpu.HBM)
    return pl.pallas_call(
        join_kernel,
        out_shape=jax.ShapeDtypeStruct((L, E, D), jnp.bfloat16),
        in_specs=[
            pl.BlockSpec(memory_space=pltpu.SMEM),
            pl.BlockSpec(memory_space=pltpu.VMEM),
            hbm,
        ],
        out_specs=hbm,
        input_output_aliases={2: 0},
        scratch_shapes=[pltpu.SemaphoreType.DMA((HALF // 2,))],
        compiler_params=pltpu.CompilerParams(vmem_limit_bytes=8 * 2**20),
        name="join_halves",
    )(core, other, full)


def moment_kernel(source_ref, near_ref, far_ref, m_ref, o_ref, ms, sem):
    copies = []
    for s in range(DEPTH):
        source = source_ref[s]
        for z in range(NZ):
            columns = slice(z * COLS, (z + 1) * COLS)
            near = near_ref[s, :, columns].astype(jnp.float32)
            far = far_ref[s, :, columns].astype(jnp.float32)
            initial = jnp.where(source == 1, near, far)
            moment = BACK_I * initial + BACK_M * m_ref[s, :, columns]
            ms[s, :, columns] = jnp.where(source > 0, moment, 0.0)
        copy = pltpu.make_async_copy(ms.at[s], o_ref.at[s], sem.at[s])
        copy.start()
        copies.append(copy)
    for copy in copies:
        copy.wait()


def update_momentum(source, near, far, momentum):
    vmem = pl.BlockSpec(memory_space=pltpu.VMEM)
    return pl.pallas_call(
        moment_kernel,
        out_shape=jax.ShapeDtypeStruct((DEPTH, E, D), jnp.float32),
        in_specs=[pl.BlockSpec(memory_space=pltpu.SMEM), vmem, vmem, vmem],
        out_specs=pl.BlockSpec(memory_space=pltpu.HBM),
        scratch_shapes=[
            pltpu.VMEM((DEPTH, E, D), jnp.float32),
            pltpu.SemaphoreType.DMA((DEPTH,)),
        ],
        compiler_params=pltpu.CompilerParams(vmem_limit_bytes=16 * 2**20),
        cost_estimate=pl.CostEstimate(
            flops=4 * 10**6, bytes_accessed=6 * 2**20, transcendentals=0
        ),
        name="update_momentum",
    )(source, near, far, momentum)


def spread(x, axis, count):
    return lax.all_to_all(jnp.broadcast_to(x[None], (count,) + x.shape), axis, 0, 0, tiled=True)


def local(grad_partial, weights, momentum, owners):
    y, x, core = lax.axis_index("y"), lax.axis_index("x"), lax.axis_index("core")
    own_index = lax.axis_index(Z)
    layers = jnp.arange(L, dtype=jnp.int32)
    first = HALF * core
    slots = jnp.sum(
        ((owners[None, :] == owners[:, None]) & (layers[None, :] < layers[:, None])).astype(
            jnp.int32
        ),
        axis=1,
    )

    kept = lax.dynamic_slice_in_dim(weights, first, HALF, 0)
    weights_half = lax.all_gather(kept, Z)

    my_layer = first + 2 * x + y // RG
    my_rows = (y % RG) * ROWS
    my_owner = lax.dynamic_index_in_dim(owners, my_layer, 0, keepdims=False)
    my_slot = lax.dynamic_index_in_dim(slots, my_layer, 0, keepdims=False)

    held = lax.dynamic_slice(momentum[0], (my_slot, my_rows, 0), (1, ROWS, D))[0]
    held = held.astype(jnp.bfloat16).reshape(ROWS, NZ, COLS).transpose(1, 0, 2)
    previous = lax.all_to_all(held, Z, 0, 0, tiled=True)
    previous = lax.dynamic_index_in_dim(previous, my_owner, 0, keepdims=False).astype(jnp.float32)

    outgoing = grad_partial[0].reshape(L * RG, ROWS, COLS)
    arrived = lax.all_to_all(outgoing, ("core", "x", "y"), 0, 0, tiled=True)
    summed = jnp.sum(arrived.astype(jnp.float32), axis=0)
    initial = INIT_S * summed + INIT_M * previous

    block = spread(initial.astype(jnp.bfloat16), Z, NZ)
    block = spread(block, "y", NY)
    ahead = [(k, (k + 1) % NX) for k in range(NX)]
    back = [(k, (k - 1) % NX) for k in range(NX)]
    left0 = lax.ppermute(block[:RG], "x", ahead)
    right1 = lax.ppermute(block[RG:], "x", back)
    left1 = lax.ppermute(block[RG:], "x", ahead)
    right0 = lax.ppermute(block[:RG], "x", back)
    far0 = lax.ppermute(left0, "x", ahead)
    far1 = lax.ppermute(right1, "x", back)

    hits = (owners[None, :] == own_index) & (
        slots[None, :] == jnp.arange(DEPTH, dtype=jnp.int32)[:, None]
    )
    present = jnp.sum(hits.astype(jnp.int32), axis=1)
    which = jnp.sum(hits.astype(jnp.int32) * layers[None, :], axis=1)
    in_half = (which >= first) & (which < first + HALF)
    source = jnp.where(present > 0, jnp.where(in_half, 1, 2), 0).astype(jnp.int32)
    far0, far1, weights_half = lax.optimization_barrier((far0, far1, weights_half))
    places = (x + jnp.array([0, NX - 1, 2, 1], jnp.int32)) % NX
    index = jnp.concatenate([places, which % HALF]).astype(jnp.int32)
    xs, near = assemble(index, block, left0, left1, far0, far1, right0, right1)

    where = core.astype(jnp.int32)[None]
    xs, near = lax.optimization_barrier((xs, near))
    xs = xs.reshape(HALF * E, D)
    far = lax.ppermute(near, "core", [(0, 1), (1, 0)])
    high, low = polynomials(xs)
    high, low, far = lax.optimization_barrier((high, low, far))
    half, full = update_weights(where, xs, high, low, weights_half)
    other = lax.ppermute(half, "core", [(0, 1), (1, 0)])
    moment = update_momentum(source, near, far, momentum[0])
    weights_out = join_halves(where, other, full)
    return (weights_out, moment[None])


def solution(mesh):
    mesh = Mesh(mesh.devices.reshape(NY, NX, NC, NZ), ("y", "x", "core", "fsdp"))
    in_specs = (
        P(DP, None, None, Z),
        P(None, None, Z),
        P(Z, None, None, None),
        P(),
    )
    out_specs = (P(), P(Z, None, None, None))
    return jax.shard_map(local, mesh=mesh, in_specs=in_specs, out_specs=out_specs, check_vma=False)
```

```python
import jax
import jax.numpy as jnp
from jax import lax
from jax.experimental import pallas as pl
from jax.experimental.pallas import tpu as pltpu
from jax.sharding import Mesh, PartitionSpec as P

E = 64
D = 2048
L = 16
DEPTH = 4
ITERS = 5
NY, NX, NC, NZ = 8, 4, 2, 16
HALF = L // NC
RG = 4
ROWS = E // RG
COLS = D // NZ
GROUP = 4 * E
DP = ("y", "x", "core")
Z = "fsdp"

coef_a = 3.4445
coef_b = -4.775
coef_c = 2.0315
moment_rate = 0.95
learn_rate = 0.1
decay_rate = 0.1
scale = 0.2 * D**0.5
INIT_S = 1.0 + moment_rate
INIT_M = moment_rate * moment_rate
BACK_I = 1.0 / INIT_S
BACK_M = moment_rate - INIT_M / INIT_S


def split(a):
    high = a.astype(jnp.bfloat16)
    return high, (a - high.astype(jnp.float32)).astype(jnp.bfloat16)


def dot(a, b):
    return jnp.dot(a, b, preferred_element_type=jnp.float32)


def assemble_kernel(index_ref, own_ref, *refs):
    *pieces, xs, near_ref = refs
    pieces = [(ref, 0, 1 + k // 2, k % 2) for k, ref in enumerate(pieces)]
    pieces += [(own_ref, part * RG, 0, part) for part in range(2)]
    for ref, at, place, part in pieces:
        layer = 2 * index_ref[place] + part
        for z in range(NZ):
            xs[layer, :, z * COLS : (z + 1) * COLS] = ref[at : at + RG, z].reshape(E, COLS)
    for s in range(DEPTH):
        near_ref[s] = xs[index_ref[NX + s]]


def assemble(index, own, *others):
    vmem = pl.BlockSpec(memory_space=pltpu.VMEM)
    return pl.pallas_call(
        assemble_kernel,
        out_shape=(
            jax.ShapeDtypeStruct((HALF, E, D), jnp.bfloat16),
            jax.ShapeDtypeStruct((DEPTH, E, D), jnp.bfloat16),
        ),
        in_specs=[pl.BlockSpec(memory_space=pltpu.SMEM), vmem] + [vmem] * len(others),
        out_specs=(vmem, vmem),
        compiler_params=pltpu.CompilerParams(vmem_limit_bytes=16 * 2**20),
        cost_estimate=pl.CostEstimate(flops=0, bytes_accessed=4 * 2**20, transcendentals=0),
        name="assemble",
    )(index, own, *others)


def poly_kernel(xs, high_ref, low_ref):
    row = lax.broadcasted_iota(jnp.int32, (GROUP, GROUP), 0)
    col = lax.broadcasted_iota(jnp.int32, (GROUP, GROUP), 1)
    same = (row >> 6) == (col >> 6)
    diagonal = row == col
    eye_a = jnp.where(diagonal, coef_a, 0.0)

    def mm(a, b):
        return dot(a[0], b[0]) + (dot(a[0], b[1]) + dot(a[1], b[0]))

    groups = range(HALF * E // GROUP)
    grams, scales = [], []
    for g in groups:
        x = xs[g * GROUP : (g + 1) * GROUP, :]
        gram = lax.dot_general(
            x, x, (((1,), (1,)), ((), ())), preferred_element_type=jnp.float32
        )
        trace = jnp.where(diagonal, gram, 0.0)
        by_row = jnp.sum(trace, axis=1, keepdims=True)
        by_col = jnp.sum(trace, axis=0, keepdims=True)
        total_row = jnp.sum(jnp.where(same, by_col, 0.0), axis=1, keepdims=True)
        total_col = jnp.sum(jnp.where(same, by_row, 0.0), axis=0, keepdims=True)
        inv_row = 1.0 / (jnp.sqrt(total_row) + 1e-07)
        inv_col = 1.0 / (jnp.sqrt(total_col) + 1e-07)
        grams.append(jnp.where(same, gram * inv_row * inv_col, 0.0))
        scales.append(inv_col)
    polys = [None for _ in groups]
    for repeat in range(ITERS):
        gram_parts = [split(gram) for gram in grams]
        squares = [mm(gram, gram) for gram in gram_parts]
        steps = [eye_a + coef_b * gram + coef_c * sq for gram, sq in zip(grams, squares)]
        step_parts = [split(step) for step in steps]
        if repeat < ITERS - 1:
            halfway = [split(mm(step, gram)) for step, gram in zip(step_parts, gram_parts)]
            grams = [mm(half, step) for half, step in zip(halfway, step_parts)]
        polys = [
            step if poly is None else mm(part, split(poly))
            for step, part, poly in zip(steps, step_parts, polys)
        ]
    for g in groups:
        high_ref[g], low_ref[g] = split(polys[g] * scales[g])


def polynomials(x):
    vmem = pl.BlockSpec(memory_space=pltpu.VMEM)
    poly = jax.ShapeDtypeStruct((HALF * E // GROUP, GROUP, GROUP), jnp.bfloat16)
    return pl.pallas_call(
        poly_kernel,
        out_shape=(poly, poly),
        in_specs=[vmem],
        out_specs=(vmem, vmem),
        compiler_params=pltpu.CompilerParams(vmem_limit_bytes=16 * 2**20),
        cost_estimate=pl.CostEstimate(
            flops=8 * 10**9, bytes_accessed=4 * 2**20, transcendentals=0
        ),
        name="polynomials",
    )(x)


def weights_kernel(xs, high_ref, low_ref, w_ref, half_ref):
    for g in range(HALF * E // GROUP):
        high, low = high_ref[g], low_ref[g]
        for z in range(NZ // 2):
            x = xs[g * GROUP : (g + 1) * GROUP, 2 * z * COLS : 2 * (z + 1) * COLS]
            ortho = dot(high, x) + dot(low, x)
            for part in range(2):
                k = 2 * z + part
                wide = w_ref[k, 4 * g : 4 * (g + 1)].reshape(GROUP, COLS).astype(jnp.float32)
                mine = ortho[:, part * COLS : (part + 1) * COLS]
                new = wide - learn_rate * (scale * mine + decay_rate * wide)
                half_ref[4 * g : 4 * (g + 1), :, k * COLS : (k + 1) * COLS] = new.astype(
                    jnp.bfloat16
                ).reshape(4, E, COLS)


def update_weights(xs, high, low, weights):
    vmem = pl.BlockSpec(memory_space=pltpu.VMEM)
    return pl.pallas_call(
        weights_kernel,
        out_shape=jax.ShapeDtypeStruct((HALF, E, D), jnp.bfloat16),
        in_specs=[vmem, vmem, vmem, vmem],
        out_specs=vmem,
        compiler_params=pltpu.CompilerParams(vmem_limit_bytes=16 * 2**20),
        cost_estimate=pl.CostEstimate(
            flops=2 * 10**9, bytes_accessed=6 * 2**20, transcendentals=0
        ),
        name="update_weights",
    )(xs, high, low, weights)


def join_kernel(core_ref, other_ref, mine_ref, full_ref, sem):
    del mine_ref
    base = (NC - 1 - core_ref[0]) * HALF
    copies = [
        pltpu.make_async_copy(
            other_ref.at[pl.ds(2 * k, 2)], full_ref.at[pl.ds(base + 2 * k, 2)], sem.at[k]
        )
        for k in range(HALF // 2)
    ]
    for copy in copies:
        copy.start()
    for copy in copies:
        copy.wait()


def join_halves(core, other, full):
    hbm = pl.BlockSpec(memory_space=pltpu.HBM)
    return pl.pallas_call(
        join_kernel,
        out_shape=jax.ShapeDtypeStruct((L, E, D), jnp.bfloat16),
        in_specs=[
            pl.BlockSpec(memory_space=pltpu.SMEM),
            pl.BlockSpec(memory_space=pltpu.VMEM),
            hbm,
        ],
        out_specs=hbm,
        input_output_aliases={2: 0},
        scratch_shapes=[pltpu.SemaphoreType.DMA((HALF // 2,))],
        compiler_params=pltpu.CompilerParams(vmem_limit_bytes=8 * 2**20),
        name="join_halves",
    )(core, other, full)


def moment_kernel(
    core_ref, source_ref, half_ref, near_ref, far_ref, m_ref, o_ref, full_ref, ms, sem, half_sem
):
    base = core_ref[0] * HALF
    copies = [
        pltpu.make_async_copy(
            half_ref.at[pl.ds(2 * k, 2)], full_ref.at[pl.ds(base + 2 * k, 2)], half_sem.at[k]
        )
        for k in range(HALF // 2)
    ]
    for copy in copies:
        copy.start()
    for s in range(DEPTH):
        source = source_ref[s]
        for z in range(NZ):
            columns = slice(z * COLS, (z + 1) * COLS)
            near = near_ref[s, :, columns].astype(jnp.float32)
            far = far_ref[s, :, columns].astype(jnp.float32)
            initial = jnp.where(source == 1, near, far)
            moment = BACK_I * initial + BACK_M * m_ref[s, :, columns]
            ms[s, :, columns] = jnp.where(source > 0, moment, 0.0)
        copy = pltpu.make_async_copy(ms.at[s], o_ref.at[s], sem.at[s])
        copy.start()
        copies.append(copy)
    for copy in copies:
        copy.wait()


def update_momentum(core, source, half, near, far, momentum):
    smem = pl.BlockSpec(memory_space=pltpu.SMEM)
    vmem = pl.BlockSpec(memory_space=pltpu.VMEM)
    hbm = pl.BlockSpec(memory_space=pltpu.HBM)
    return pl.pallas_call(
        moment_kernel,
        out_shape=(
            jax.ShapeDtypeStruct((DEPTH, E, D), jnp.float32),
            jax.ShapeDtypeStruct((L, E, D), jnp.bfloat16),
        ),
        in_specs=[smem, smem, vmem, vmem, vmem, vmem],
        out_specs=(hbm, hbm),
        scratch_shapes=[
            pltpu.VMEM((DEPTH, E, D), jnp.float32),
            pltpu.SemaphoreType.DMA((DEPTH,)),
            pltpu.SemaphoreType.DMA((HALF // 2,)),
        ],
        compiler_params=pltpu.CompilerParams(vmem_limit_bytes=16 * 2**20),
        cost_estimate=pl.CostEstimate(
            flops=4 * 10**6, bytes_accessed=10 * 2**20, transcendentals=0
        ),
        name="update_momentum",
    )(core, source, half, near, far, momentum)


def spread(x, axis, count):
    return lax.all_to_all(jnp.broadcast_to(x[None], (count,) + x.shape), axis, 0, 0, tiled=True)


def local(grad_partial, weights, momentum, owners):
    y, x, core = lax.axis_index("y"), lax.axis_index("x"), lax.axis_index("core")
    own_index = lax.axis_index(Z)
    layers = jnp.arange(L, dtype=jnp.int32)
    first = HALF * core
    slots = jnp.sum(
        ((owners[None, :] == owners[:, None]) & (layers[None, :] < layers[:, None])).astype(
            jnp.int32
        ),
        axis=1,
    )

    kept = lax.dynamic_slice_in_dim(weights, first, HALF, 0)
    weights_half = lax.all_gather(kept, Z)

    my_layer = first + 2 * x + y // RG
    my_rows = (y % RG) * ROWS
    my_owner = lax.dynamic_index_in_dim(owners, my_layer, 0, keepdims=False)
    my_slot = lax.dynamic_index_in_dim(slots, my_layer, 0, keepdims=False)

    held = lax.dynamic_slice(momentum[0], (my_slot, my_rows, 0), (1, ROWS, D))[0]
    held = held.astype(jnp.bfloat16).reshape(ROWS, NZ, COLS).transpose(1, 0, 2)
    previous = lax.all_to_all(held, Z, 0, 0, tiled=True)
    previous = lax.dynamic_index_in_dim(previous, my_owner, 0, keepdims=False).astype(jnp.float32)

    outgoing = grad_partial[0].reshape(L * RG, ROWS, COLS)
    arrived = lax.all_to_all(outgoing, ("core", "x", "y"), 0, 0, tiled=True)
    summed = jnp.sum(arrived.astype(jnp.float32), axis=0)
    initial = INIT_S * summed + INIT_M * previous

    block = spread(initial.astype(jnp.bfloat16), Z, NZ)
    block = spread(block, "y", NY)
    ahead = [(k, (k + 1) % NX) for k in range(NX)]
    back = [(k, (k - 1) % NX) for k in range(NX)]
    left0 = lax.ppermute(block[:RG], "x", ahead)
    right1 = lax.ppermute(block[RG:], "x", back)
    left0, second_half = lax.optimization_barrier((left0, block[RG:]))
    far0 = lax.ppermute(left0, "x", ahead)
    left1 = lax.ppermute(second_half, "x", ahead)
    right1, first_half = lax.optimization_barrier((right1, block[:RG]))
    far1 = lax.ppermute(right1, "x", back)
    right0 = lax.ppermute(first_half, "x", back)

    hits = (owners[None, :] == own_index) & (
        slots[None, :] == jnp.arange(DEPTH, dtype=jnp.int32)[:, None]
    )
    present = jnp.sum(hits.astype(jnp.int32), axis=1)
    which = jnp.sum(hits.astype(jnp.int32) * layers[None, :], axis=1)
    in_half = (which >= first) & (which < first + HALF)
    source = jnp.where(present > 0, jnp.where(in_half, 1, 2), 0).astype(jnp.int32)
    far0, far1, weights_half = lax.optimization_barrier((far0, far1, weights_half))
    places = (x + jnp.array([0, NX - 1, 2, 1], jnp.int32)) % NX
    index = jnp.concatenate([places, which % HALF]).astype(jnp.int32)
    xs, near = assemble(index, block, left0, left1, far0, far1, right0, right1)

    where = core.astype(jnp.int32)[None]
    xs, near = lax.optimization_barrier((xs, near))
    xs = xs.reshape(HALF * E, D)
    far = lax.ppermute(near, "core", [(0, 1), (1, 0)])
    high, low = polynomials(xs)
    high, low, far = lax.optimization_barrier((high, low, far))
    half = update_weights(xs, high, low, weights_half)
    other = lax.ppermute(half, "core", [(0, 1), (1, 0)])
    moment, full = update_momentum(where, source, half, near, far, momentum[0])
    weights_out = join_halves(where, other, full)
    return (weights_out, moment[None])


def solution(mesh):
    mesh = Mesh(mesh.devices.reshape(NY, NX, NC, NZ), ("y", "x", "core", "fsdp"))
    in_specs = (
        P(DP, None, None, Z),
        P(None, None, Z),
        P(Z, None, None, None),
        P(),
    )
    out_specs = (P(), P(Z, None, None, None))
    return jax.shard_map(local, mesh=mesh, in_specs=in_specs, out_specs=out_specs, check_vma=False)
```

```python
import jax
import jax.numpy as jnp
from jax import lax
from jax.experimental import pallas as pl
from jax.experimental.pallas import tpu as pltpu
from jax.sharding import Mesh, PartitionSpec as P

E = 64
D = 2048
L = 16
DEPTH = 4
ITERS = 5
NY, NX, NC, NZ = 8, 4, 2, 16
HALF = L // NC
RG = 4
ROWS = E // RG
COLS = D // NZ
GROUP = 4 * E
DP = ("y", "x", "core")
Z = "fsdp"

coef_a = 3.4445
coef_b = -4.775
coef_c = 2.0315
moment_rate = 0.95
learn_rate = 0.1
decay_rate = 0.1
scale = 0.2 * D**0.5
INIT_S = 1.0 + moment_rate
INIT_M = moment_rate * moment_rate
BACK_I = 1.0 / INIT_S
BACK_M = moment_rate - INIT_M / INIT_S


def split(a):
    high = a.astype(jnp.bfloat16)
    return high, (a - high.astype(jnp.float32)).astype(jnp.bfloat16)


def dot(a, b):
    return jnp.dot(a, b, preferred_element_type=jnp.float32)


def assemble_kernel(index_ref, own_ref, *refs):
    *pieces, xs, near_ref = refs
    pieces = [(ref, 0, 1 + k // 2, k % 2) for k, ref in enumerate(pieces)]
    pieces += [(own_ref, part * RG, 0, part) for part in range(2)]
    for ref, at, place, part in pieces:
        layer = 2 * index_ref[place] + part
        for z in range(NZ):
            xs[layer, :, z * COLS : (z + 1) * COLS] = ref[at : at + RG, z].reshape(E, COLS)
    for s in range(DEPTH):
        near_ref[s] = xs[index_ref[NX + s]]


def assemble(index, own, *others):
    vmem = pl.BlockSpec(memory_space=pltpu.VMEM)
    return pl.pallas_call(
        assemble_kernel,
        out_shape=(
            jax.ShapeDtypeStruct((HALF, E, D), jnp.bfloat16),
            jax.ShapeDtypeStruct((DEPTH, E, D), jnp.bfloat16),
        ),
        in_specs=[pl.BlockSpec(memory_space=pltpu.SMEM), vmem] + [vmem] * len(others),
        out_specs=(vmem, vmem),
        compiler_params=pltpu.CompilerParams(vmem_limit_bytes=16 * 2**20),
        cost_estimate=pl.CostEstimate(flops=0, bytes_accessed=4 * 2**20, transcendentals=0),
        name="assemble",
    )(index, own, *others)


def poly_kernel(xs, high_ref, low_ref):
    row = lax.broadcasted_iota(jnp.int32, (GROUP, GROUP), 0)
    col = lax.broadcasted_iota(jnp.int32, (GROUP, GROUP), 1)
    same = (row >> 6) == (col >> 6)
    diagonal = row == col
    eye_a = jnp.where(diagonal, coef_a, 0.0)

    def mm(a, b):
        return dot(a[0], b[0]) + (dot(a[0], b[1]) + dot(a[1], b[0]))

    groups = range(HALF * E // GROUP)
    grams, scales = [], []
    for g in groups:
        x = xs[g * GROUP : (g + 1) * GROUP, :]
        gram = lax.dot_general(
            x, x, (((1,), (1,)), ((), ())), preferred_element_type=jnp.float32
        )
        trace = jnp.where(diagonal, gram, 0.0)
        by_row = jnp.sum(trace, axis=1, keepdims=True)
        by_col = jnp.sum(trace, axis=0, keepdims=True)
        total_row = jnp.sum(jnp.where(same, by_col, 0.0), axis=1, keepdims=True)
        total_col = jnp.sum(jnp.where(same, by_row, 0.0), axis=0, keepdims=True)
        inv_row = 1.0 / (jnp.sqrt(total_row) + 1e-07)
        inv_col = 1.0 / (jnp.sqrt(total_col) + 1e-07)
        grams.append(jnp.where(same, gram * inv_row * inv_col, 0.0))
        scales.append(inv_col)
    polys = [None for _ in groups]
    for repeat in range(ITERS):
        gram_parts = [split(gram) for gram in grams]
        squares = [mm(gram, gram) for gram in gram_parts]
        steps = [eye_a + coef_b * gram + coef_c * sq for gram, sq in zip(grams, squares)]
        step_parts = [split(step) for step in steps]
        if repeat < ITERS - 1:
            halfway = [split(mm(step, gram)) for step, gram in zip(step_parts, gram_parts)]
            grams = [mm(half, step) for half, step in zip(halfway, step_parts)]
        polys = [
            step if poly is None else mm(part, split(poly))
            for step, part, poly in zip(steps, step_parts, polys)
        ]
    for g in groups:
        high_ref[g], low_ref[g] = split(polys[g] * scales[g])


def polynomials(x):
    vmem = pl.BlockSpec(memory_space=pltpu.VMEM)
    poly = jax.ShapeDtypeStruct((HALF * E // GROUP, GROUP, GROUP), jnp.bfloat16)
    return pl.pallas_call(
        poly_kernel,
        out_shape=(poly, poly),
        in_specs=[vmem],
        out_specs=(vmem, vmem),
        compiler_params=pltpu.CompilerParams(vmem_limit_bytes=16 * 2**20),
        cost_estimate=pl.CostEstimate(
            flops=8 * 10**9, bytes_accessed=4 * 2**20, transcendentals=0
        ),
        name="polynomials",
    )(x)


def weights_kernel(xs, high_ref, low_ref, w_ref, half_ref):
    for g in range(HALF * E // GROUP):
        high, low = high_ref[g], low_ref[g]
        for z in range(NZ // 2):
            x = xs[g * GROUP : (g + 1) * GROUP, 2 * z * COLS : 2 * (z + 1) * COLS]
            ortho = dot(high, x) + dot(low, x)
            for part in range(2):
                k = 2 * z + part
                wide = w_ref[k, 4 * g : 4 * (g + 1)].reshape(GROUP, COLS).astype(jnp.float32)
                mine = ortho[:, part * COLS : (part + 1) * COLS]
                new = wide - learn_rate * (scale * mine + decay_rate * wide)
                half_ref[4 * g : 4 * (g + 1), :, k * COLS : (k + 1) * COLS] = new.astype(
                    jnp.bfloat16
                ).reshape(4, E, COLS)


def update_weights(xs, high, low, weights):
    vmem = pl.BlockSpec(memory_space=pltpu.VMEM)
    return pl.pallas_call(
        weights_kernel,
        out_shape=jax.ShapeDtypeStruct((HALF, E, D), jnp.bfloat16),
        in_specs=[vmem, vmem, vmem, vmem],
        out_specs=vmem,
        compiler_params=pltpu.CompilerParams(vmem_limit_bytes=16 * 2**20),
        cost_estimate=pl.CostEstimate(
            flops=2 * 10**9, bytes_accessed=6 * 2**20, transcendentals=0
        ),
        name="update_weights",
    )(xs, high, low, weights)


def join_kernel(core_ref, other_ref, mine_ref, full_ref, sem):
    del mine_ref
    base = (NC - 1 - core_ref[0]) * HALF
    copies = [
        pltpu.make_async_copy(
            other_ref.at[pl.ds(2 * k, 2)], full_ref.at[pl.ds(base + 2 * k, 2)], sem.at[k]
        )
        for k in range(HALF // 2)
    ]
    for copy in copies:
        copy.start()
    for copy in copies:
        copy.wait()


def join_halves(core, other, full):
    hbm = pl.BlockSpec(memory_space=pltpu.HBM)
    return pl.pallas_call(
        join_kernel,
        out_shape=jax.ShapeDtypeStruct((L, E, D), jnp.bfloat16),
        in_specs=[
            pl.BlockSpec(memory_space=pltpu.SMEM),
            pl.BlockSpec(memory_space=pltpu.VMEM),
            hbm,
        ],
        out_specs=hbm,
        input_output_aliases={2: 0},
        scratch_shapes=[pltpu.SemaphoreType.DMA((HALF // 2,))],
        compiler_params=pltpu.CompilerParams(vmem_limit_bytes=8 * 2**20),
        name="join_halves",
    )(core, other, full)


def moment_kernel(
    core_ref, source_ref, half_ref, near_ref, far_ref, m_ref, o_ref, full_ref, ms, sem, half_sem
):
    base = core_ref[0] * HALF
    copies = [
        pltpu.make_async_copy(
            half_ref.at[pl.ds(2 * k, 2)], full_ref.at[pl.ds(base + 2 * k, 2)], half_sem.at[k]
        )
        for k in range(HALF // 2)
    ]
    for copy in copies:
        copy.start()
    for s in range(DEPTH):
        source = source_ref[s]
        for z in range(NZ):
            columns = slice(z * COLS, (z + 1) * COLS)
            near = near_ref[s, :, columns].astype(jnp.float32)
            far = far_ref[s, :, columns].astype(jnp.float32)
            initial = jnp.where(source == 1, near, far)
            moment = BACK_I * initial + BACK_M * m_ref[s, :, columns]
            ms[s, :, columns] = jnp.where(source > 0, moment, 0.0)
        copy = pltpu.make_async_copy(ms.at[s], o_ref.at[s], sem.at[s])
        copy.start()
        copies.append(copy)
    for copy in copies:
        copy.wait()


def update_momentum(core, source, half, near, far, momentum):
    smem = pl.BlockSpec(memory_space=pltpu.SMEM)
    vmem = pl.BlockSpec(memory_space=pltpu.VMEM)
    hbm = pl.BlockSpec(memory_space=pltpu.HBM)
    return pl.pallas_call(
        moment_kernel,
        out_shape=(
            jax.ShapeDtypeStruct((DEPTH, E, D), jnp.float32),
            jax.ShapeDtypeStruct((L, E, D), jnp.bfloat16),
        ),
        in_specs=[smem, smem, vmem, vmem, vmem, vmem],
        out_specs=(hbm, hbm),
        scratch_shapes=[
            pltpu.VMEM((DEPTH, E, D), jnp.float32),
            pltpu.SemaphoreType.DMA((DEPTH,)),
            pltpu.SemaphoreType.DMA((HALF // 2,)),
        ],
        compiler_params=pltpu.CompilerParams(vmem_limit_bytes=16 * 2**20),
        cost_estimate=pl.CostEstimate(
            flops=4 * 10**6, bytes_accessed=10 * 2**20, transcendentals=0
        ),
        name="update_momentum",
    )(core, source, half, near, far, momentum)


def spread(x, axis, count):
    return lax.all_to_all(jnp.broadcast_to(x[None], (count,) + x.shape), axis, 0, 0, tiled=True)


def local(grad_partial, weights, momentum, owners):
    y, x, core = lax.axis_index("y"), lax.axis_index("x"), lax.axis_index("core")
    own_index = lax.axis_index(Z)
    layers = jnp.arange(L, dtype=jnp.int32)
    first = HALF * core
    slots = jnp.sum(
        ((owners[None, :] == owners[:, None]) & (layers[None, :] < layers[:, None])).astype(
            jnp.int32
        ),
        axis=1,
    )

    kept = lax.dynamic_slice_in_dim(weights, first, HALF, 0)
    weights_half = lax.all_gather(kept, Z)

    my_layer = first + 2 * x + y // RG
    my_rows = (y % RG) * ROWS
    my_owner = lax.dynamic_index_in_dim(owners, my_layer, 0, keepdims=False)
    my_slot = lax.dynamic_index_in_dim(slots, my_layer, 0, keepdims=False)

    held = lax.dynamic_slice(momentum[0], (my_slot, my_rows, 0), (1, ROWS, D))[0]
    held = held.astype(jnp.bfloat16).reshape(ROWS, NZ, COLS).transpose(1, 0, 2)
    previous = lax.all_to_all(held, Z, 0, 0, tiled=True)
    previous = lax.dynamic_index_in_dim(previous, my_owner, 0, keepdims=False).astype(jnp.float32)

    outgoing = grad_partial[0].reshape(L * RG, ROWS, COLS)
    arrived = lax.all_to_all(outgoing, ("core", "x", "y"), 0, 0, tiled=True)
    summed = jnp.sum(arrived.astype(jnp.float32), axis=0)
    initial = INIT_S * summed + INIT_M * previous

    block = spread(initial.astype(jnp.bfloat16), Z, NZ)
    block = spread(block, "y", NY)
    ahead = [(k, (k + 1) % NX) for k in range(NX)]
    back = [(k, (k - 1) % NX) for k in range(NX)]
    left0 = lax.ppermute(block[:RG], "x", ahead)
    right1 = lax.ppermute(block[RG:], "x", back)
    left1 = lax.ppermute(block[RG:], "x", ahead)
    right0 = lax.ppermute(block[:RG], "x", back)
    far0 = lax.ppermute(left0, "x", ahead)
    far1 = lax.ppermute(right1, "x", back)

    hits = (owners[None, :] == own_index) & (
        slots[None, :] == jnp.arange(DEPTH, dtype=jnp.int32)[:, None]
    )
    present = jnp.sum(hits.astype(jnp.int32), axis=1)
    which = jnp.sum(hits.astype(jnp.int32) * layers[None, :], axis=1)
    in_half = (which >= first) & (which < first + HALF)
    source = jnp.where(present > 0, jnp.where(in_half, 1, 2), 0).astype(jnp.int32)
    far0, far1, weights_half = lax.optimization_barrier((far0, far1, weights_half))
    places = (x + jnp.array([0, NX - 1, 2, 1], jnp.int32)) % NX
    index = jnp.concatenate([places, which % HALF]).astype(jnp.int32)
    xs, near = assemble(index, block, left0, left1, far0, far1, right0, right1)

    where = core.astype(jnp.int32)[None]
    xs, near = lax.optimization_barrier((xs, near))
    xs = xs.reshape(HALF * E, D)
    far = lax.ppermute(near, "core", [(0, 1), (1, 0)])
    high, low = polynomials(xs)
    high, low, far = lax.optimization_barrier((high, low, far))
    half = update_weights(xs, high, low, weights_half)
    other = lax.ppermute(half, "core", [(0, 1), (1, 0)])
    moment, full = update_momentum(where, source, half, near, far, momentum[0])
    weights_out = join_halves(where, other, full)
    return (weights_out, moment[None])


def solution(mesh):
    mesh = Mesh(mesh.devices.reshape(NY, NX, NC, NZ), ("y", "x", "core", "fsdp"))
    in_specs = (
        P(DP, None, None, Z),
        P(None, None, Z),
        P(Z, None, None, None),
        P(),
    )
    out_specs = (P(), P(Z, None, None, None))
    return jax.shard_map(local, mesh=mesh, in_specs=in_specs, out_specs=out_specs, check_vma=False)
```

```python
import jax
import jax.numpy as jnp
from jax import lax
from jax.experimental import pallas as pl
from jax.experimental.pallas import tpu as pltpu
from jax.sharding import Mesh, PartitionSpec as P

E = 64
D = 2048
L = 16
DEPTH = 4
ITERS = 5
NY, NX, NC, NZ = 8, 4, 2, 16
HALF = L // NC
RG = 4
ROWS = E // RG
COLS = D // NZ
GROUP = 4 * E
DP = ("y", "x", "core")
Z = "fsdp"

coef_a = 3.4445
coef_b = -4.775
coef_c = 2.0315
moment_rate = 0.95
learn_rate = 0.1
decay_rate = 0.1
scale = 0.2 * D**0.5
INIT_S = 1.0 + moment_rate
INIT_M = moment_rate * moment_rate
BACK_I = 1.0 / INIT_S
BACK_M = moment_rate - INIT_M / INIT_S


def split(a):
    high = a.astype(jnp.bfloat16)
    return high, (a - high.astype(jnp.float32)).astype(jnp.bfloat16)


def dot(a, b):
    return jnp.dot(a, b, preferred_element_type=jnp.float32)


def assemble_kernel(index_ref, own_ref, *refs):
    *pieces, xs, near_ref = refs
    pieces = [(ref, 0, 1 + k // 2, k % 2) for k, ref in enumerate(pieces)]
    pieces += [(own_ref, part * RG, 0, part) for part in range(2)]
    for ref, at, place, part in pieces:
        layer = 2 * index_ref[place] + part
        for z in range(NZ):
            xs[layer, :, z * COLS : (z + 1) * COLS] = ref[at : at + RG, z].reshape(E, COLS)
    for s in range(DEPTH):
        near_ref[s] = xs[index_ref[NX + s]]


def assemble(index, own, *others):
    vmem = pl.BlockSpec(memory_space=pltpu.VMEM)
    return pl.pallas_call(
        assemble_kernel,
        out_shape=(
            jax.ShapeDtypeStruct((HALF, E, D), jnp.bfloat16),
            jax.ShapeDtypeStruct((DEPTH, E, D), jnp.bfloat16),
        ),
        in_specs=[pl.BlockSpec(memory_space=pltpu.SMEM), vmem] + [vmem] * len(others),
        out_specs=(vmem, vmem),
        compiler_params=pltpu.CompilerParams(vmem_limit_bytes=16 * 2**20),
        cost_estimate=pl.CostEstimate(flops=0, bytes_accessed=4 * 2**20, transcendentals=0),
        name="assemble",
    )(index, own, *others)


def poly_kernel(xs, high_ref, low_ref):
    row = lax.broadcasted_iota(jnp.int32, (GROUP, GROUP), 0)
    col = lax.broadcasted_iota(jnp.int32, (GROUP, GROUP), 1)
    same = (row >> 6) == (col >> 6)
    diagonal = row == col
    eye_a = jnp.where(diagonal, coef_a, 0.0)

    def mm(a, b):
        return dot(a[0], b[0]) + (dot(a[0], b[1]) + dot(a[1], b[0]))

    groups = range(HALF * E // GROUP)
    grams, scales = [], []
    for g in groups:
        x = xs[g * GROUP : (g + 1) * GROUP, :]
        gram = lax.dot_general(
            x, x, (((1,), (1,)), ((), ())), preferred_element_type=jnp.float32
        )
        trace = jnp.where(diagonal, gram, 0.0)
        by_row = jnp.sum(trace, axis=1, keepdims=True)
        by_col = jnp.sum(trace, axis=0, keepdims=True)
        total_row = jnp.sum(jnp.where(same, by_col, 0.0), axis=1, keepdims=True)
        total_col = jnp.sum(jnp.where(same, by_row, 0.0), axis=0, keepdims=True)
        inv_row = 1.0 / (jnp.sqrt(total_row) + 1e-07)
        inv_col = 1.0 / (jnp.sqrt(total_col) + 1e-07)
        grams.append(jnp.where(same, gram * inv_row * inv_col, 0.0))
        scales.append(inv_col)
    polys = [None for _ in groups]
    for repeat in range(ITERS):
        gram_parts = [split(gram) for gram in grams]
        squares = [mm(gram, gram) for gram in gram_parts]
        steps = [eye_a + coef_b * gram + coef_c * sq for gram, sq in zip(grams, squares)]
        step_parts = [split(step) for step in steps]
        if repeat < ITERS - 1:
            halfway = [split(mm(step, gram)) for step, gram in zip(step_parts, gram_parts)]
            grams = [mm(half, step) for half, step in zip(halfway, step_parts)]
        polys = [
            step if poly is None else mm(part, split(poly))
            for step, part, poly in zip(steps, step_parts, polys)
        ]
    for g in groups:
        high_ref[g], low_ref[g] = split(polys[g] * scales[g])


def polynomials(x):
    vmem = pl.BlockSpec(memory_space=pltpu.VMEM)
    poly = jax.ShapeDtypeStruct((HALF * E // GROUP, GROUP, GROUP), jnp.bfloat16)
    return pl.pallas_call(
        poly_kernel,
        out_shape=(poly, poly),
        in_specs=[vmem],
        out_specs=(vmem, vmem),
        compiler_params=pltpu.CompilerParams(vmem_limit_bytes=16 * 2**20),
        cost_estimate=pl.CostEstimate(
            flops=8 * 10**9, bytes_accessed=4 * 2**20, transcendentals=0
        ),
        name="polynomials",
    )(x)


def weights_kernel(xs, high_ref, low_ref, w_ref, half_ref):
    for g in range(HALF * E // GROUP):
        high, low = high_ref[g], low_ref[g]
        for z in range(NZ // 2):
            x = xs[g * GROUP : (g + 1) * GROUP, 2 * z * COLS : 2 * (z + 1) * COLS]
            ortho = dot(high, x) + dot(low, x)
            for part in range(2):
                k = 2 * z + part
                wide = w_ref[k, 4 * g : 4 * (g + 1)].reshape(GROUP, COLS).astype(jnp.float32)
                mine = ortho[:, part * COLS : (part + 1) * COLS]
                new = wide - learn_rate * (scale * mine + decay_rate * wide)
                half_ref[4 * g : 4 * (g + 1), :, k * COLS : (k + 1) * COLS] = new.astype(
                    jnp.bfloat16
                ).reshape(4, E, COLS)


def update_weights(xs, high, low, weights):
    vmem = pl.BlockSpec(memory_space=pltpu.VMEM)
    return pl.pallas_call(
        weights_kernel,
        out_shape=jax.ShapeDtypeStruct((HALF, E, D), jnp.bfloat16),
        in_specs=[vmem, vmem, vmem, vmem],
        out_specs=vmem,
        compiler_params=pltpu.CompilerParams(vmem_limit_bytes=16 * 2**20),
        cost_estimate=pl.CostEstimate(
            flops=2 * 10**9, bytes_accessed=6 * 2**20, transcendentals=0
        ),
        name="update_weights",
    )(xs, high, low, weights)


def join_kernel(core_ref, other_ref, mine_ref, full_ref, sem):
    del mine_ref
    base = (NC - 1 - core_ref[0]) * HALF
    copies = [
        pltpu.make_async_copy(
            other_ref.at[pl.ds(2 * k, 2)], full_ref.at[pl.ds(base + 2 * k, 2)], sem.at[k]
        )
        for k in range(HALF // 2)
    ]
    for copy in copies:
        copy.start()
    for copy in copies:
        copy.wait()


def join_halves(core, other, full):
    hbm = pl.BlockSpec(memory_space=pltpu.HBM)
    return pl.pallas_call(
        join_kernel,
        out_shape=jax.ShapeDtypeStruct((L, E, D), jnp.bfloat16),
        in_specs=[
            pl.BlockSpec(memory_space=pltpu.SMEM),
            pl.BlockSpec(memory_space=pltpu.VMEM),
            hbm,
        ],
        out_specs=hbm,
        input_output_aliases={2: 0},
        scratch_shapes=[pltpu.SemaphoreType.DMA((HALF // 2,))],
        compiler_params=pltpu.CompilerParams(vmem_limit_bytes=8 * 2**20),
        name="join_halves",
    )(core, other, full)


def moment_kernel(
    core_ref, source_ref, half_ref, near_ref, far_ref, m_ref, o_ref, full_ref, ms, sem, half_sem
):
    base = core_ref[0] * HALF
    copies = [
        pltpu.make_async_copy(
            half_ref.at[pl.ds(2 * k, 2)], full_ref.at[pl.ds(base + 2 * k, 2)], half_sem.at[k]
        )
        for k in range(HALF // 2)
    ]
    for copy in copies:
        copy.start()
    for s in range(DEPTH):
        source = source_ref[s]
        for z in range(NZ):
            columns = slice(z * COLS, (z + 1) * COLS)
            near = near_ref[s, :, columns].astype(jnp.float32)
            far = far_ref[s, :, columns].astype(jnp.float32)
            initial = jnp.where(source == 1, near, far)
            moment = BACK_I * initial + BACK_M * m_ref[s, :, columns]
            ms[s, :, columns] = jnp.where(source > 0, moment, 0.0)
        copy = pltpu.make_async_copy(ms.at[s], o_ref.at[s], sem.at[s])
        copy.start()
        copies.append(copy)
    for copy in copies:
        copy.wait()


def update_momentum(core, source, half, near, far, momentum):
    smem = pl.BlockSpec(memory_space=pltpu.SMEM)
    vmem = pl.BlockSpec(memory_space=pltpu.VMEM)
    hbm = pl.BlockSpec(memory_space=pltpu.HBM)
    return pl.pallas_call(
        moment_kernel,
        out_shape=(
            jax.ShapeDtypeStruct((DEPTH, E, D), jnp.float32),
            jax.ShapeDtypeStruct((L, E, D), jnp.bfloat16),
        ),
        in_specs=[smem, smem, vmem, vmem, vmem, vmem],
        out_specs=(hbm, hbm),
        scratch_shapes=[
            pltpu.VMEM((DEPTH, E, D), jnp.float32),
            pltpu.SemaphoreType.DMA((DEPTH,)),
            pltpu.SemaphoreType.DMA((HALF // 2,)),
        ],
        compiler_params=pltpu.CompilerParams(vmem_limit_bytes=16 * 2**20),
        cost_estimate=pl.CostEstimate(
            flops=4 * 10**6, bytes_accessed=10 * 2**20, transcendentals=0
        ),
        name="update_momentum",
    )(core, source, half, near, far, momentum)


def spread(x, axis, count):
    return lax.all_to_all(jnp.broadcast_to(x[None], (count,) + x.shape), axis, 0, 0, tiled=True)


def local(grad_partial, weights, momentum, owners):
    y, x, core = lax.axis_index("y"), lax.axis_index("x"), lax.axis_index("core")
    own_index = lax.axis_index(Z)
    layers = jnp.arange(L, dtype=jnp.int32)
    first = HALF * core
    slots = jnp.sum(
        ((owners[None, :] == owners[:, None]) & (layers[None, :] < layers[:, None])).astype(
            jnp.int32
        ),
        axis=1,
    )

    kept = lax.dynamic_slice_in_dim(weights, first, HALF, 0)
    weights_half = lax.all_gather(kept, Z)

    my_layer = first + 2 * x + y // RG
    my_rows = (y % RG) * ROWS
    my_owner = lax.dynamic_index_in_dim(owners, my_layer, 0, keepdims=False)
    my_slot = lax.dynamic_index_in_dim(slots, my_layer, 0, keepdims=False)

    held = lax.dynamic_slice(momentum[0], (my_slot, my_rows, 0), (1, ROWS, D))[0]
    held = held.astype(jnp.bfloat16).reshape(ROWS, NZ, COLS).transpose(1, 0, 2)
    previous = lax.all_to_all(held, Z, 0, 0, tiled=True)
    previous = lax.dynamic_index_in_dim(previous, my_owner, 0, keepdims=False).astype(jnp.float32)

    outgoing = grad_partial[0].reshape(L * RG, ROWS, COLS)
    arrived = lax.all_to_all(outgoing, ("core", "x", "y"), 0, 0, tiled=True)
    summed = jnp.sum(arrived.astype(jnp.float32), axis=0)
    initial = INIT_S * summed + INIT_M * previous

    block = spread(initial.astype(jnp.bfloat16), Z, NZ)
    block = spread(block, "y", NY)
    ring = [(k, c, 1 - 2 * c) for k in range(NX) for c in range(NC)]
    ahead = [(NC * k + c, NC * ((k + way) % NX) + c) for k, c, way in ring]
    back = [(NC * k + c, NC * ((k - way) % NX) + c) for k, c, way in ring]
    left0 = lax.ppermute(block[:RG], ("x", "core"), ahead)
    right1 = lax.ppermute(block[RG:], ("x", "core"), back)
    left1 = lax.ppermute(block[RG:], ("x", "core"), ahead)
    right0 = lax.ppermute(block[:RG], ("x", "core"), back)
    far0 = lax.ppermute(left0, ("x", "core"), ahead)
    far1 = lax.ppermute(right1, ("x", "core"), back)

    hits = (owners[None, :] == own_index) & (
        slots[None, :] == jnp.arange(DEPTH, dtype=jnp.int32)[:, None]
    )
    present = jnp.sum(hits.astype(jnp.int32), axis=1)
    which = jnp.sum(hits.astype(jnp.int32) * layers[None, :], axis=1)
    in_half = (which >= first) & (which < first + HALF)
    source = jnp.where(present > 0, jnp.where(in_half, 1, 2), 0).astype(jnp.int32)
    far0, far1, weights_half = lax.optimization_barrier((far0, far1, weights_half))
    places = (x + (1 - 2 * core) * jnp.array([0, -1, 2, 1], jnp.int32) + NX) % NX
    index = jnp.concatenate([places, which % HALF]).astype(jnp.int32)
    xs, near = assemble(index, block, left0, left1, far0, far1, right0, right1)

    where = core.astype(jnp.int32)[None]
    xs, near = lax.optimization_barrier((xs, near))
    xs = xs.reshape(HALF * E, D)
    far = lax.ppermute(near, "core", [(0, 1), (1, 0)])
    high, low = polynomials(xs)
    high, low, far = lax.optimization_barrier((high, low, far))
    half = update_weights(xs, high, low, weights_half)
    other = lax.ppermute(half, "core", [(0, 1), (1, 0)])
    moment, full = update_momentum(where, source, half, near, far, momentum[0])
    weights_out = join_halves(where, other, full)
    return (weights_out, moment[None])


def solution(mesh):
    mesh = Mesh(mesh.devices.reshape(NY, NX, NC, NZ), ("y", "x", "core", "fsdp"))
    in_specs = (
        P(DP, None, None, Z),
        P(None, None, Z),
        P(Z, None, None, None),
        P(),
    )
    out_specs = (P(), P(Z, None, None, None))
    return jax.shard_map(local, mesh=mesh, in_specs=in_specs, out_specs=out_specs, check_vma=False)
```
